256 devices in a mesh: pipe: 8 (over y_lo, x), expert: 32 (over z, y_hi, core).
Axes of the slice: x: 4, y: 4 (y_hi: 2, y_lo: 2; y = y_hi * 2 + y_lo), z: 8, core: 2. Of those that a mesh axis runs over, the one named last changes fastest.
Arguments:
- fwd_input: bfloat16 [8, 2048, 2048], P('pipe', 'expert'), may hold values from -6 to 6
- fwd_routes: int32 [8, 2048, 8], P('pipe', 'expert'), may hold values from 0 to 63, all different within a row; in each aligned block of 64 rows (0 to 63, 64 to 127, ..., all dimensions but the last counted through in order) at most 10 rows name the same one
- fwd_gates: float32 [8, 2048, 8], P('pipe', 'expert'), may hold values from 0.03 to 0.3
- bwd_input: bfloat16 [8, 2048, 2048], P('pipe', 'expert'), may hold values from -6 to 6
- bwd_grad: bfloat16 [8, 2048, 2048], P('pipe', 'expert'), may hold values from -6 to 6
- bwd_routes: int32 [8, 2048, 8], P('pipe', 'expert'), may hold values from 0 to 63, all different within a row; in each aligned block of 64 rows (0 to 63, 64 to 127, ..., all dimensions but the last counted through in order) at most 10 rows name the same one
- bwd_gates: float32 [8, 2048, 8], P('pipe', 'expert'), may hold values from 0.03 to 0.3
- w_in: bfloat16 [8, 64, 2048, 768], P('pipe', 'expert'), may hold values from -0.125 to 0.125
- w_out: bfloat16 [8, 64, 768, 2048], P('pipe', 'expert'), may hold values from -0.21875 to 0.21875
Outputs:
- next_forward: bfloat16 [8, 2048, 2048], P('pipe', 'expert')
- next_cotangent: bfloat16 [8, 2048, 2048], P('pipe', 'expert')
The draws below stay inside these ranges and needn't reach their ends.
Inputs may be any that keep to these rules, and one draw needn't show every extreme that they name: `fwd_routes`: each row names 8 different experts. In each aligned block of 64 rows (the rows of one device) no expert is named by more than 10 rows, a bound that some block reaches. `bwd_routes`: each row names 8 different experts. In each aligned block of 64 rows (the rows of one device) no expert is named by more than 10 rows, a bound that some block reaches.
All inputs are finite; a program needn't handle non-finite values.
Results may differ from the reference program's by a relative error of at most 0.006.
Values may be sent and summed in bfloat16 or wider, within the bound.
No kernel may reach another device: no remote copies, remote signals or barrier semaphores. Data moves between devices by JAX's collectives and lax.ppermute only.
A program may use at most 128 MiB of HBM per device.

```python
import math
import jax
import jax.numpy as jnp
import numpy as np
from jax import lax

D = 2048
H = 768
EXPERTS = 64
TOP = 8
TOK_DEV = 64
CAP = 10
TOKENS = 2048
N_PIPE = 8
N_EXPERT = 32


def levels(key, dims, shards, low, top_value):
    factor_of, own = 1.0, jax.random.fold_in(key, 6)
    for dim, shards_of in shards:
        steps = jnp.exp(jax.random.uniform(jax.random.fold_in(own, dim), (shards_of,), jnp.float32, low / len(shards), top_value / len(shards)))
        factor_of = factor_of * jnp.repeat(steps, dims[dim] // shards_of).reshape([-1 if axis == dim else 1 for axis in range(len(dims))])
    return factor_of


def assign_block(own_key, own, number, rows, amount, top, most, skew):
    order = jax.random.permutation(own_key, amount)
    packed, usual = shares(amount, rows * top, most, skew, True), shares(amount, rows * top, most, skew, False)
    places = jnp.arange(amount)

    def named(tallies, turn):
        used = int((tallies > 0).sum())
        fixed = max(1, used // 4)
        shifted = fixed + (places - fixed + turn * (used - fixed)) % max(1, amount - fixed)
        return jnp.zeros((amount,), jnp.int32).at[order[jnp.where(places < fixed, places, shifted)]].set(jnp.asarray(tallies, jnp.int32))

    tallies = jnp.where(number % 4 == 0, named(packed, number // 4), named(usual, number - number // 4 - 1))
    mixed = jax.random.permutation(jax.random.fold_in(own, 3), amount)
    donor, taker = mixed[0:amount // 2 * 2:2], mixed[1:amount // 2 * 2:2]
    room = jnp.minimum(tallies[donor] - 1, most - tallies[taker]) // 2
    room = jnp.where((donor == order[0]) | (taker == order[0]) | (tallies[taker] == 0), 0, jnp.maximum(room, 0))
    shifted = jax.random.randint(jax.random.fold_in(own, 4), (amount // 2,), 0, 1 << 20) % (room + 1)
    tallies = tallies.at[donor].add(-shifted).at[taker].add(shifted)
    items = jnp.searchsorted(jnp.cumsum(tallies), jnp.arange(rows * top), side="right").astype(jnp.int32)
    listing = items.reshape(top, rows).T
    listing = listing[jax.random.permutation(jax.random.fold_in(own, 1), rows)]
    turn = jax.random.randint(jax.random.fold_in(own, 2), (rows, 1), 0, top)
    return jnp.take_along_axis(listing, (jnp.arange(top)[None, :] + turn) % top, axis=1)


def shares(number_of, total, bound, skew, full):
    portions = [(1 << 20) // math.isqrt(grade ** skew) + 1 for grade in range(1, number_of + 1)]
    largest = bound if full else min(bound, max(-(-total // number_of), total * portions[0] // sum(portions)))
    least = 1 if total - largest >= number_of - 1 else 0
    holding, rest = [largest] + [least] * (number_of - 1), total - largest - least * (number_of - 1)
    while rest > 0:
        candidates = [i for i in range(1, number_of) if holding[i] < largest] or [i for i in range(1, number_of) if holding[i] < bound]
        mass, remaining = sum([portions[i] for i in candidates]), rest
        for i in candidates:
            extra = min(bound - holding[i], max(1, remaining * portions[i] // mass), rest)
            holding[i] = holding[i] + extra
            rest = rest - extra
    return np.array(holding)


def scatter_about(own_key, extent, deviation, bound, cuts=(), dtype=jnp.bfloat16):
    entries = jax.random.normal(own_key, extent, jnp.float32) * deviation
    if len(cuts) > 0:
        entries = levels(own_key, extent, cuts, -0.22, 0.18) * entries
    return jnp.clip(entries, min=-bound, max=bound).astype(dtype)


def setup_inputs(seed: int = 0) -> dict:
    splits = jax.random.split(jax.random.key(seed), 10)
    fwd_input = scatter_about(splits[0], (N_PIPE, TOKENS, D), 1.0, 6.0, ((0, 8), (1, 32)))
    fwd_routes_keys = jax.random.split(jax.random.fold_in(splits[1], 1), N_PIPE * TOKENS // TOK_DEV)
    fwd_routes_turns = jax.random.permutation(jax.random.fold_in(splits[1], 3), N_PIPE * TOKENS // TOK_DEV)
    fwd_routes = jax.vmap(lambda own, number: assign_block(jax.random.fold_in(splits[1], 2), own, number, TOK_DEV, EXPERTS, TOP, CAP, 2))(fwd_routes_keys, fwd_routes_turns).reshape((N_PIPE, TOKENS, TOP))
    fwd_gates = jnp.clip(jnp.exp(math.log(0.3) - 2.3025852 * jax.random.uniform(splits[2], (N_PIPE, TOKENS, TOP), jnp.float32) ** levels(splits[2], (N_PIPE, TOKENS, TOP), ((0, 8), (1, 32)), -0.2, 0.2)), 0.03, 0.3)
    bwd_input = scatter_about(splits[3], (N_PIPE, TOKENS, D), 1.0, 6.0, ((0, 8), (1, 32)))
    bwd_grad = scatter_about(splits[4], (N_PIPE, TOKENS, D), 1.0, 6.0, ((0, 8), (1, 32)))
    bwd_routes_keys = jax.random.split(jax.random.fold_in(splits[5], 1), N_PIPE * TOKENS // TOK_DEV)
    bwd_routes_turns = jax.random.permutation(jax.random.fold_in(splits[5], 3), N_PIPE * TOKENS // TOK_DEV)
    bwd_routes = jax.vmap(lambda own, number: assign_block(jax.random.fold_in(splits[5], 2), own, number, TOK_DEV, EXPERTS, TOP, CAP, 2))(bwd_routes_keys, bwd_routes_turns).reshape((N_PIPE, TOKENS, TOP))
    bwd_gates = jnp.clip(jnp.exp(math.log(0.3) - 2.3025852 * jax.random.uniform(splits[6], (N_PIPE, TOKENS, TOP), jnp.float32) ** levels(splits[6], (N_PIPE, TOKENS, TOP), ((0, 8), (1, 32)), -0.2, 0.2)), 0.03, 0.3)
    w_in = scatter_about(splits[7], (N_PIPE, EXPERTS, D, H), D ** -0.5, 0.125, ((0, 8), (1, 32)))
    w_out = scatter_about(splits[8], (N_PIPE, EXPERTS, H, D), H ** -0.5, 0.21875, ((0, 8), (1, 32)))
    return dict(fwd_input=fwd_input, fwd_routes=fwd_routes, fwd_gates=fwd_gates, bwd_input=bwd_input, bwd_grad=bwd_grad, bwd_routes=bwd_routes, bwd_gates=bwd_gates, w_in=w_in, w_out=w_out)


def silu_slope(values):
    sigma = jax.nn.sigmoid(values)
    return sigma * (1.0 + values * (1.0 - sigma))


def section_pass(inputs, grads, routes, gates, weight_in, weight_out, backward):
    flat_routes = routes.reshape(-1)
    flat_gates = gates.reshape(-1)
    largest = N_EXPERT * CAP

    def one_expert(total, expert):
        hits = flat_routes == expert
        where_hit = jnp.nonzero(hits, size=largest, fill_value=0)[0].astype(jnp.int32)
        valid = jnp.arange(largest) < jnp.sum(hits.astype(jnp.int32))
        token_ids = where_hit // TOP
        in_rows = inputs[token_ids]
        pre_act = jnp.dot(in_rows, weight_in[expert], preferred_element_type=jnp.float32)
        if backward:
            grad_rows = grads[token_ids]
            hidden_grad = jnp.dot(grad_rows, weight_out[expert].T, preferred_element_type=jnp.float32)
            pre_grad = (hidden_grad * silu_slope(pre_act)).astype(jnp.bfloat16)
            result = jnp.dot(pre_grad, weight_in[expert].T, preferred_element_type=jnp.float32).astype(jnp.bfloat16)
        else:
            hidden = jax.nn.silu(pre_act).astype(jnp.bfloat16)
            result = jnp.dot(hidden, weight_out[expert], preferred_element_type=jnp.float32).astype(jnp.bfloat16)
        scale = jnp.where(valid, flat_gates[where_hit], 0.0)
        total = total.at[token_ids].add(scale[:, None] * result.astype(jnp.float32))
        return total, None

    start = jnp.zeros((inputs.shape[0], inputs.shape[1]), jnp.float32)
    total, _ = lax.scan(one_expert, start, jnp.arange(EXPERTS))
    base = grads if backward else inputs
    return (base.astype(jnp.float32) + total).astype(jnp.bfloat16)


def reference(fwd_input, fwd_routes, fwd_gates, bwd_input, bwd_grad, bwd_routes, bwd_gates, w_in, w_out):
    fwd_list = []
    bwd_list = []
    for section in range(N_PIPE):
        fwd_list.append(section_pass(fwd_input[section], fwd_input[section], fwd_routes[section], fwd_gates[section], w_in[section], w_out[section], False))
        bwd_list.append(section_pass(bwd_input[section], bwd_grad[section], bwd_routes[section], bwd_gates[section], w_in[section], w_out[section], True))
    fwd_out = jnp.stack(fwd_list)
    bwd_out = jnp.stack(bwd_list)
    blank = jnp.zeros_like(fwd_out[:1])
    next_forward = jnp.concatenate([blank, fwd_out[:-1]], axis=0)
    next_cotangent = jnp.concatenate([bwd_out[1:], blank], axis=0)
    return next_forward, next_cotangent
```

```python
import jax
import jax.numpy as jnp
from jax import lax
from jax.sharding import PartitionSpec as P

TOP = 8
CAP = 10
EXPERT = "expert"
NEAR = (1, -1, 2, -2)
FAR = (0, 3, -3, 4)


def ring_pairs(by, count):
    return [(i, ((i // 4 + by) % (count // 4)) * 4 + i % 4) for i in range(count)]


def along_z(value, by):
    return lax.ppermute(value, EXPERT, ring_pairs(by, lax.axis_size(EXPERT)))


def swap(value, bit):
    return lax.ppermute(value, EXPERT, [(i, i ^ bit) for i in range(lax.axis_size(EXPERT))])


def swap_y(value):
    return swap(value, 2)


def swap_c(value):
    return swap(value, 1)


def shifted(value, axis, by):
    count = lax.axis_size(axis)
    pairs = [(i, i + by) for i in range(count) if 0 <= i + by < count]
    return lax.ppermute(value, axis, pairs)


def silu_slope(values):
    sigma = jax.nn.sigmoid(values)
    return sigma * (1.0 + values * (1.0 - sigma))


def gathered_tables(routes, gates):
    count = lax.axis_size(EXPERT)
    groups = [[4 * z + i for z in range(count // 4)] for i in range(4)]
    own = jnp.concatenate([routes.T.astype(jnp.float32), gates.T], axis=0)
    every = lax.all_gather(own, EXPERT, axis_index_groups=groups)
    mine = lax.axis_index(EXPERT) // 4
    order = (mine - jnp.array(NEAR + FAR, dtype=jnp.int32)) % (count // 4)
    return jnp.take(every, order, axis=0).reshape(len(order), 2, TOP, -1)


def slot_tables(tables):
    tokens = tables.shape[-1]
    me = lax.axis_index(EXPERT)
    near = jnp.array([me, me ^ 1, me ^ 2, me ^ 3], dtype=jnp.int32)
    ids = (near[:, None] * 2 + jnp.arange(2, dtype=jnp.int32)[None, :]).reshape(-1)
    flat = tables.reshape(2, 4, 2, TOP, tokens).transpose(0, 2, 3, 1, 4).reshape(2, 2, TOP, 4 * tokens)
    hits = flat[:, 0][:, None] == ids.astype(jnp.float32)[None, :, None, None]
    named = jnp.any(hits, axis=2)
    gate = jnp.sum(jnp.where(hits, flat[:, 1][:, None], 0.0), axis=2)
    place = jnp.arange(4 * tokens, dtype=jnp.int32)
    before = (place[:, None] < place[None, :]) & (place[:, None] // tokens == place[None, :] // tokens)
    position = jnp.einsum(
        "hxt,tu->hxu", named.astype(jnp.bfloat16), before.astype(jnp.bfloat16), preferred_element_type=jnp.float32
    ).astype(jnp.int32)
    slot = jnp.where(named, position + (place // tokens * CAP)[None, None, :], -1)
    match = slot[:, :, None, :] == jnp.arange(4 * CAP, dtype=jnp.int32)[None, None, :, None]
    match = match.reshape(2, 8 * 4 * CAP, 4 * tokens)
    select = match.astype(jnp.bfloat16)
    weight = jnp.where(match, jnp.repeat(gate, 4 * CAP, axis=1), 0.0)
    high = weight.astype(jnp.bfloat16)
    low = (weight - high.astype(jnp.float32)).astype(jnp.bfloat16)
    return select, jnp.concatenate([high, low], axis=1)


def gather_ring(own):
    half = own.shape[0] // 2
    up, down = {0: own}, {0: own}
    for k in (1, 2, 3):
        up[k] = along_z(up[k - 1], 1)
        down[k] = along_z(down[k - 1], -1)
    last = jnp.concatenate([along_z(up[3][:half], 1), along_z(down[3][half:], -1)], axis=0)
    return (
        jnp.concatenate([up[1], down[1], up[2], down[2]], axis=0),
        jnp.concatenate([own, up[3], down[3], last], axis=0),
    )


def dispatch(select, own):
    width = own.shape[1]
    parts = []
    for chosen, block in zip(select, gather_ring(own)):
        slots = jnp.dot(chosen, block, preferred_element_type=jnp.float32).astype(jnp.bfloat16)
        part = slots.shape[0] // 4
        here = slots[: 2 * part]
        across = swap_y(slots[2 * part :])
        parts += [here[:part], across[:part], swap_c(here[part:]), swap_c(across[part:])]
    return jnp.concatenate([p.reshape(2, 4 * CAP, width) for p in parts], axis=1)


def give_back(weights, results):
    sums = {}
    rows = 4 * CAP
    for half, offsets in ((1, FAR), (0, NEAR)):
        here, across, here_c, across_c = (
            results[:, (4 * half + i) * rows : (4 * half + i + 1) * rows].reshape(2 * rows, -1) for i in range(4)
        )
        returned = swap_y(jnp.concatenate([across, swap_c(across_c)], axis=0))
        every = jnp.concatenate([here, swap_c(here_c), returned], axis=0)
        every = jnp.concatenate([every, every], axis=0)
        total = lax.dot_general(
            weights[half], every, (((0,), (0,)), ((), ())), preferred_element_type=jnp.float32
        ).astype(jnp.bfloat16)
        tokens = total.shape[0] // 4
        for i, k in enumerate(offsets):
            sums[k] = total[i * tokens : (i + 1) * tokens]
    return sums


def added(one, two):
    return (one.astype(jnp.float32) + two.astype(jnp.float32)).astype(jnp.bfloat16)


def scatter_ring(sums, base):
    half = base.shape[0] // 2
    down = along_z(sums[4][:half], -1)
    up = along_z(sums[4][half:], 1)
    down = jnp.concatenate([added(sums[3][:half], down), sums[3][half:]], axis=0)
    up = jnp.concatenate([sums[-3][:half], added(sums[-3][half:], up)], axis=0)
    for k in (2, 1):
        down = added(sums[k], along_z(down, -1))
        up = added(sums[-k], along_z(up, 1))
    down = along_z(down, -1)
    up = along_z(up, 1)
    whole = base.astype(jnp.float32) + sums[0].astype(jnp.float32)
    return (whole + down.astype(jnp.float32) + up.astype(jnp.float32)).astype(jnp.bfloat16)


def expert_forward(rows, weight_in, weight_out):
    pre_act = jnp.einsum("jrd,jdh->jrh", rows, weight_in, preferred_element_type=jnp.float32)
    hidden = jax.nn.silu(pre_act).astype(jnp.bfloat16)
    result = jnp.einsum("jrh,jhd->jrd", hidden, weight_out, preferred_element_type=jnp.float32)
    return result.astype(jnp.bfloat16)


def expert_backward(rows, grads, weight_in, weight_out):
    pre_act = jnp.einsum("jrd,jdh->jrh", rows, weight_in, preferred_element_type=jnp.float32)
    hidden_grad = jnp.einsum("jrd,jhd->jrh", grads, weight_out, preferred_element_type=jnp.float32)
    pre_grad = (hidden_grad * silu_slope(pre_act)).astype(jnp.bfloat16)
    result = jnp.einsum("jrh,jdh->jrd", pre_grad, weight_in, preferred_element_type=jnp.float32)
    return result.astype(jnp.bfloat16)


def per_device(
    fwd_input, fwd_routes, fwd_gates, bwd_input, bwd_grad, bwd_routes, bwd_gates, w_in, w_out
):
    weight_in = w_in[0]
    weight_out = w_out[0]
    width = fwd_input.shape[2]
    fwd_select, fwd_weights = slot_tables(gathered_tables(fwd_routes[0], fwd_gates[0]))
    bwd_select, bwd_weights = slot_tables(gathered_tables(bwd_routes[0], bwd_gates[0]))
    fwd_rows = dispatch(fwd_select, fwd_input[0])
    bwd_rows = dispatch(bwd_select, jnp.concatenate([bwd_input[0], bwd_grad[0]], axis=1))
    fwd_result = expert_forward(fwd_rows, weight_in, weight_out)
    fwd_out = scatter_ring(give_back(fwd_weights, fwd_result), fwd_input[0])
    next_forward = shifted(fwd_out[None], "pipe", 1)
    bwd_result = expert_backward(bwd_rows[..., :width], bwd_rows[..., width:], weight_in, weight_out)
    bwd_out = scatter_ring(give_back(bwd_weights, bwd_result), bwd_grad[0])
    next_cotangent = shifted(bwd_out[None], "pipe", -1)
    return (next_forward, next_cotangent)


def solution(mesh):
    rows = P("pipe", "expert", None)
    weights = P("pipe", "expert", None, None)
    return jax.shard_map(
        per_device,
        mesh=mesh,
        in_specs=(rows,) * 7 + (weights,) * 2,
        out_specs=(rows, rows),
        check_vma=False,
    )
```

```python
import functools

import jax
import jax.numpy as jnp
from jax import lax
from jax.experimental import pallas as pl
from jax.experimental.pallas import tpu as pltpu
from jax.sharding import PartitionSpec as P

TOP = 8
CAP = 10
EXPERT = "expert"
NEAR = (1, -1, 2, -2)
FAR = (0, 3, -3, 4)
FOUR = 4
PART = 2 * FOUR * CAP
ALIGNED = 48
META = 128
VMEM = pl.BlockSpec(memory_space=pltpu.VMEM)
LIMIT = 48 << 20


def along_z(value, by):
    count = lax.axis_size(EXPERT)
    return lax.ppermute(value, EXPERT, [(i, ((i // 4 + by) % (count // 4)) * 4 + i % 4) for i in range(count)])


def swap(value, bits):
    return lax.ppermute(value, EXPERT, [(i, i ^ bits) for i in range(lax.axis_size(EXPERT))])


def shifted(value, axis, by):
    count = lax.axis_size(axis)
    pairs = [(i, i + by) for i in range(count) if 0 <= i + by < count]
    return lax.ppermute(value, axis, pairs)


def stage(*values):
    return lax.optimization_barrier(values)


def silu_slope(values):
    sigma = jax.nn.sigmoid(values)
    return sigma * (1.0 + values * (1.0 - sigma))


def diagonal(rows):
    row = lax.broadcasted_iota(jnp.int32, (rows, META), 0)
    return jnp.where(row == lax.broadcasted_iota(jnp.int32, (rows, META), 1), 1.0, 0.0).astype(jnp.bfloat16)


def pack_kernel(x, g, f_routes, f_gates, b_routes, b_gates, out):
    rows = []
    for routes, gates in ((b_routes, b_gates), (f_routes, f_gates)):
        rows.append(routes[...].astype(jnp.float32))
        rest = gates[...]
        for _ in range(3):
            part = rest.astype(jnp.bfloat16).astype(jnp.float32)
            rows.append(part)
            rest = rest - part
    table = jnp.concatenate(rows, axis=0).astype(jnp.bfloat16)
    width = x.shape[1]
    out[:, :width] = x[...]
    out[:, width : 2 * width] = g[...]
    meta = lax.dot_general(
        table, diagonal(8 * TOP), (((0,), (0,)), ((), ())), preferred_element_type=jnp.float32
    )
    out[:, 2 * width :] = meta.astype(jnp.bfloat16)


def pack(x, g, f_routes, f_gates, b_routes, b_gates):
    return pl.pallas_call(
        pack_kernel,
        out_shape=jax.ShapeDtypeStruct((x.shape[0], 2 * x.shape[1] + META), jnp.bfloat16),
        in_specs=[VMEM] * 6,
        out_specs=VMEM,
        compiler_params=pltpu.CompilerParams(vmem_limit_bytes=LIMIT),
        name="pack",
    )(x, g, f_routes.T, f_gates.T, b_routes.T, b_gates.T)


def unpack(blocks):
    meta = jnp.concatenate([b[:, b.shape[1] - META :] for b in blocks], axis=0)
    rows = lax.dot_general(
        diagonal(8 * TOP), meta, (((1,), (1,)), ((), ())), preferred_element_type=jnp.float32
    )
    both = []
    for start in (0, 4 * TOP):
        part = [rows[start + i * TOP : start + (i + 1) * TOP] for i in range(4)]
        both.append((part[0], part[1] + part[2] + part[3]))
    return both


def select_rows(ids, routes, gates, weights, select):
    lanes = routes.shape[1]
    tokens = lanes // FOUR
    row = lax.broadcasted_iota(jnp.int32, (2 * FOUR, lanes), 0)
    named = jnp.zeros((2 * FOUR, lanes), jnp.float32)
    gate = jnp.zeros((2 * FOUR, lanes), jnp.float32)
    for x in range(2 * FOUR):
        hit = routes == ids[x].astype(jnp.float32)
        named = jnp.where(row == x, jnp.max(jnp.where(hit, 1.0, 0.0), axis=0, keepdims=True), named)
        gate = jnp.where(row == x, jnp.sum(jnp.where(hit, gates, 0.0), axis=0, keepdims=True), gate)
    first = lax.broadcasted_iota(jnp.int32, (lanes, lanes), 0)
    second = lax.broadcasted_iota(jnp.int32, (lanes, lanes), 1)
    before = jnp.where((first < second) & (first // tokens == second // tokens), 1.0, 0.0).astype(jnp.bfloat16)
    position = jnp.dot(named.astype(jnp.bfloat16), before, preferred_element_type=jnp.float32)
    source = lax.broadcasted_iota(jnp.int32, (2 * FOUR, lanes), 1) // tokens
    slot = jnp.where(named > 0.5, position + (source * CAP).astype(jnp.float32), -1.0)
    place = lax.broadcasted_iota(jnp.int32, (PART, lanes), 0)
    early = place < PART // 2
    place = jnp.where(early, place, place - PART // 2).astype(jnp.float32)
    for a in range(FOUR):
        match = jnp.where(early, slot[2 * a : 2 * a + 1], slot[2 * a + 1 : 2 * a + 2]) == place
        weight = jnp.where(match, jnp.where(early, gate[2 * a : 2 * a + 1], gate[2 * a + 1 : 2 * a + 2]), 0.0)
        high = weight.astype(jnp.bfloat16)
        select[a * PART : (a + 1) * PART, :] = jnp.where(match, 1.0, 0.0).astype(jnp.bfloat16)
        weights[a * PART : (a + 1) * PART, :] = high
        weights[(FOUR + a) * PART : (FOUR + a + 1) * PART, :] = (weight - high.astype(jnp.float32)).astype(jnp.bfloat16)


def spread(chosen, four, outs, first):
    tile = 512
    for i in range(outs[0].shape[1] // tile):
        at = slice(i * tile, (i + 1) * tile)
        block = jnp.concatenate([b[:, at] for b in four], axis=0)
        slots = jnp.dot(chosen, block, preferred_element_type=jnp.float32)
        for a in range(FOUR):
            outs[a][first : first + PART, at] = slots[a * PART : (a + 1) * PART].astype(jnp.bfloat16)


def pick_backward_kernel(ids, b0, b1, b2, b3, p0, p1, p2, p3, weights, tables, select):
    blocks = (b0, b1, b2, b3)
    (routes, gates), (other_routes, other_gates) = unpack(blocks)
    tables[:TOP, :] = other_routes
    tables[TOP:, :] = other_gates
    select_rows(ids, routes, gates, weights, select)
    spread(select[...], blocks, (p0, p1, p2, p3), 0)


def pick_forward_kernel(ids, *refs):
    blocks, outs, select = refs[:10], refs[10:-1], refs[-1]
    for half in range(2):
        tables, *four = blocks[5 * half : 5 * half + 5]
        select_rows(ids, tables[:TOP, :], tables[TOP:, :], outs[FOUR + half], select)
        spread(select[...], four, outs[:FOUR], half * PART)


def pick(kernel, ids, blocks, rows, width, extra):
    lanes = FOUR * blocks[-1].shape[0]
    out_shape = [jax.ShapeDtypeStruct((rows, width), jnp.bfloat16)] * FOUR
    out_shape += [jax.ShapeDtypeStruct((count, lanes), dtype) for count, dtype in extra]
    outs = pl.pallas_call(
        kernel,
        out_shape=out_shape,
        in_specs=[pl.BlockSpec(memory_space=pltpu.SMEM)] + [VMEM] * len(blocks),
        out_specs=[VMEM] * len(out_shape),
        scratch_shapes=[pltpu.VMEM((FOUR * PART, lanes), jnp.bfloat16)],
        compiler_params=pltpu.CompilerParams(vmem_limit_bytes=LIMIT),
        cost_estimate=pl.CostEstimate(flops=8 * rows * lanes * width, bytes_accessed=1 << 22, transcendentals=0),
        name="pick",
    )(ids, *blocks)
    return list(outs[:FOUR]), *outs[FOUR:]


def pick_backward(ids, blocks, width):
    extra = [(2 * FOUR * PART, jnp.bfloat16), (2 * TOP, jnp.float32)]
    return pick(pick_backward_kernel, ids, blocks, PART, width, extra)


def pick_forward(ids, near, far):
    extra = [(2 * FOUR * PART, jnp.bfloat16)] * 2
    return pick(pick_forward_kernel, ids, (*near, *far), 2 * PART, near[1].shape[1], extra)


def line_up(parts, j, rows):
    start = 0 if j == 0 else PART - ALIGNED
    for i, part in enumerate(parts):
        rows[i * ALIGNED : (i + 1) * ALIGNED, :] = part[start : start + ALIGNED, :]


def lay_out(results, outs):
    edge = PART // 2 // 16 * 16
    for i, out in enumerate(outs):
        at = i * ALIGNED
        out[:edge, :] = results[0, at : at + edge, :]
        low, high = results[0, at + edge : at + edge + 16, :], results[1, at : at + 16, :]
        row = lax.broadcasted_iota(jnp.int32, low.shape, 0)
        mixed = jnp.where(row < PART // 2 - edge, low.astype(jnp.float32), high.astype(jnp.float32))
        out[edge : edge + 16, :] = mixed.astype(jnp.bfloat16)
        out[edge + 16 :, :] = results[1, at + 16 : at + ALIGNED, :]


def tiles(total, tile, body):
    def step(i, _):
        body(pl.ds(pl.multiple_of(i * tile, tile), tile))
        return 0

    lax.fori_loop(0, total // tile, step, 0)


def half_rows(refs, half):
    return [ref.at[pl.ds(half * PART, PART), :] for ref in refs]


def forward_kernel(*refs):
    w_in, w_out, *outs, rows, hidden, results = refs[4:]
    parts = half_rows(refs[:4], 0) + half_rows(refs[:4], 1)
    for j in range(2):
        line_up(parts, j, rows)

        def into(at):
            pre = jnp.dot(rows[...], w_in[j, :, at], preferred_element_type=jnp.float32)
            hidden[:, at] = (pre * jax.nn.sigmoid(pre)).astype(jnp.bfloat16)

        def outof(at):
            out = jnp.dot(hidden[...], w_out[j, :, at], preferred_element_type=jnp.float32)
            results[j, :, at] = out.astype(jnp.bfloat16)

        tiles(hidden.shape[1], 256, into)
        tiles(rows.shape[1], 512, outof)
    lay_out(results, outs)


def backward_kernel(*refs):
    w_in, w_out, *outs, rows, grad_rows, hidden, results = refs[8:]
    width = rows.shape[1]
    parts = [ref.at[:, pl.ds(0, width)] for ref in refs[:8]]
    grads = [ref.at[:, pl.ds(width, width)] for ref in refs[:8]]
    outs = half_rows(outs, 0) + half_rows(outs, 1)
    across = (((1,), (1,)), ((), ()))
    for j in range(2):
        line_up(parts, j, rows)
        line_up(grads, j, grad_rows)

        def into(at):
            pre = jnp.dot(rows[...], w_in[j, :, at], preferred_element_type=jnp.float32)
            grad = lax.dot_general(grad_rows[...], w_out[j, at, :], across, preferred_element_type=jnp.float32)
            hidden[:, at] = (grad * silu_slope(pre)).astype(jnp.bfloat16)

        def outof(at):
            out = lax.dot_general(hidden[...], w_in[j, at, :], across, preferred_element_type=jnp.float32)
            results[j, :, at] = out.astype(jnp.bfloat16)

        tiles(hidden.shape[1], 256, into)
        tiles(rows.shape[1], 512, outof)
    lay_out(results, outs)


def experts(kernel, arrays, inputs, out_rows, weight_in, weight_out):
    width = weight_in.shape[1]
    rows = 8 * ALIGNED
    outs = 8 * PART // out_rows
    flops = 2 * (arrays + 1) * 2 * rows * width * weight_in.shape[2]
    return pl.pallas_call(
        kernel,
        out_shape=[jax.ShapeDtypeStruct((out_rows, width), jnp.bfloat16)] * outs,
        in_specs=[VMEM] * (len(inputs) + 2),
        out_specs=[VMEM] * outs,
        scratch_shapes=[pltpu.VMEM((rows, width), jnp.bfloat16)] * arrays
        + [pltpu.VMEM((rows, weight_in.shape[2]), jnp.bfloat16), pltpu.VMEM((2, rows, width), jnp.bfloat16)],
        compiler_params=pltpu.CompilerParams(vmem_limit_bytes=LIMIT),
        cost_estimate=pl.CostEstimate(flops=flops, bytes_accessed=1 << 24, transcendentals=1 << 19),
        name="experts",
    )(*inputs, weight_in, weight_out)


def gated_kernel(half, weights, p0, p1, p2, p3, s0, s1, s2, s3, every):
    for a, part in enumerate((p0, p1, p2, p3)):
        every[a * PART : (a + 1) * PART, :] = part[half * PART : (half + 1) * PART, :]
    down = (((0,), (0,)), ((), ()))
    tokens = s0.shape[0]
    tile = 512
    for i in range(every.shape[1] // tile):
        at = slice(i * tile, (i + 1) * tile)
        total = lax.dot_general(weights[: FOUR * PART, :], every[:, at], down, preferred_element_type=jnp.float32)
        total += lax.dot_general(weights[FOUR * PART :, :], every[:, at], down, preferred_element_type=jnp.float32)
        for k, out in enumerate((s0, s1, s2, s3)):
            out[:, at] = total[k * tokens : (k + 1) * tokens].astype(jnp.bfloat16)


def gated(weights, parts, half=0):
    width = parts[0].shape[1]
    tokens = weights.shape[1] // FOUR
    return pl.pallas_call(
        functools.partial(gated_kernel, half),
        out_shape=[jax.ShapeDtypeStruct((tokens, width), jnp.bfloat16)] * FOUR,
        in_specs=[VMEM] * 5,
        out_specs=[VMEM] * FOUR,
        scratch_shapes=[pltpu.VMEM((FOUR * PART, width), jnp.bfloat16)],
        compiler_params=pltpu.CompilerParams(vmem_limit_bytes=LIMIT),
        cost_estimate=pl.CostEstimate(flops=4 * 320 * 256 * width, bytes_accessed=1 << 22, transcendentals=0),
        name="gated",
    )(weights, *parts)


def hop(up, down):
    return along_z(up, 1), along_z(down, -1)


def far_hop(up, down):
    half = up.shape[0] // 2
    return along_z(up[:half], 1), along_z(down[half:], -1)


def added(one, two):
    return (one.astype(jnp.float32) + two.astype(jnp.float32)).astype(jnp.bfloat16)


def turn_back(last):
    half = last.shape[0] // 2
    return along_z(last[half:], 1), along_z(last[:half], -1)


def add_halves(up, down, pair):
    half = up.shape[0] // 2
    up = jnp.concatenate([up[:half], added(up[half:], pair[0])], axis=0)
    down = jnp.concatenate([added(down[:half], pair[1]), down[half:]], axis=0)
    return up, down


def finished(base, own, pair):
    total = base.astype(jnp.float32) + own.astype(jnp.float32)
    return (total + pair[0].astype(jnp.float32) + pair[1].astype(jnp.float32)).astype(jnp.bfloat16)


def exchange(parts):
    return [parts[0]] + [swap(parts[a], a) for a in (1, 2, 3)]


def per_device(
    fwd_input, fwd_routes, fwd_gates, bwd_input, bwd_grad, bwd_routes, bwd_gates, w_in, w_out
):
    weight_in, weight_out = w_in[0], w_out[0]
    f_own = fwd_input[0]
    width = f_own.shape[1]
    me = lax.axis_index(EXPERT)
    ids = jnp.stack([2 * (me ^ a) + j for a in range(4) for j in range(2)]).astype(jnp.int32)
    b_own = pack(bwd_input[0], bwd_grad[0], fwd_routes[0], fwd_gates[0], bwd_routes[0], bwd_gates[0])

    b1 = stage(*hop(b_own, b_own))
    b2 = stage(*hop(*b1))
    b_parts1, b_weights1, near = pick_backward(ids, (*b1, *b2), 2 * width)
    b2, b_parts1, f_own = stage(b2, b_parts1, f_own)

    b_got1 = exchange(b_parts1)
    b3 = hop(*b2)
    b4 = far_hop(*b3)
    f1 = hop(f_own, f_own)
    b_got1, b3, b4, f1 = stage(b_got1, b3, b4, f1)
    b_parts2, b_weights2, far = pick_backward(ids, (b_own, *b3, jnp.concatenate(b4, axis=0)), 2 * width)
    b_parts2, f1 = stage(b_parts2, f1)

    b_got2 = exchange(b_parts2)
    f2 = hop(*f1)
    f3 = hop(*f2)
    f4 = far_hop(*f3)
    b_got2, f2, f3, f4 = stage(b_got2, f2, f3, f4)
    f_parts, f_weights1, f_weights2 = pick_forward(
        ids, (near, *f1, *f2), (far, f_own, *f3, jnp.concatenate(f4, axis=0))
    )
    f_parts, b_got1, b_got2 = stage(f_parts, b_got1, b_got2)

    f_got = exchange(f_parts)
    b_out = experts(backward_kernel, 2, b_got1 + b_got2, 2 * PART, weight_in, weight_out)
    f_got, b_out = stage(f_got, b_out)

    b_back = exchange(b_out)
    f_out = experts(forward_kernel, 1, f_got, PART, weight_in, weight_out)
    b_back, f_out = stage(b_back, f_out)

    f_back2 = exchange(f_out[4:])
    f_core1 = swap(f_out[1], 1)
    b_sums2 = gated(b_weights2, b_back, 1)
    b_pair = turn_back(b_sums2[3])
    b_pair = hop(*add_halves(b_sums2[2], b_sums2[1], b_pair))
    b_sums1 = gated(b_weights1, b_back, 0)
    f_back2, b_pair, b_sums1, f_core1, f_back1 = stage(f_back2, b_pair, b_sums1, f_core1, f_out[:4])

    f_back1 = [f_back1[0], f_core1, swap(f_back1[2], 2), swap(f_back1[3], 3)]
    b_pair = hop(added(b_sums1[3], b_pair[0]), added(b_sums1[2], b_pair[1]))
    f_sums2 = gated(f_weights2, f_back2)
    f_pair = turn_back(f_sums2[3])
    b_pair, f_pair, f_sums2 = stage(b_pair, f_pair, f_sums2)
    b_pair = hop(added(b_sums1[1], b_pair[0]), added(b_sums1[0], b_pair[1]))
    f_pair = hop(*add_halves(f_sums2[2], f_sums2[1], f_pair))
    f_back1, b_pair, f_pair = stage(f_back1, b_pair, f_pair)

    f_sums1 = gated(f_weights1, f_back1)
    f_pair = hop(added(f_sums1[3], f_pair[0]), added(f_sums1[2], f_pair[1]))
    next_cotangent = shifted(finished(bwd_grad[0], b_sums2[0], b_pair)[None], "pipe", -1)
    f_pair, next_cotangent = stage(f_pair, next_cotangent)
    f_pair = hop(added(f_sums1[1], f_pair[0]), added(f_sums1[0], f_pair[1]))
    next_forward = shifted(finished(fwd_input[0], f_sums2[0], f_pair)[None], "pipe", 1)
    return (next_forward, next_cotangent)


def solution(mesh):
    rows = P("pipe", "expert", None)
    weights = P("pipe", "expert", None, None)
    return jax.shard_map(
        per_device,
        mesh=mesh,
        in_specs=(rows,) * 7 + (weights,) * 2,
        out_specs=(rows, rows),
        check_vma=False,
    )
```

```python
import functools

import jax
import jax.numpy as jnp
from jax import lax
from jax.experimental import pallas as pl
from jax.experimental.pallas import tpu as pltpu
from jax.sharding import PartitionSpec as P

TOP = 8
CAP = 10
EXPERT = "expert"
NEAR = (1, -1, 2, -2)
FAR = (0, 3, -3, 4)
FOUR = 4
PART = 2 * FOUR * CAP
ALIGNED = 48
META = 128
VMEM = pl.BlockSpec(memory_space=pltpu.VMEM)
LIMIT = 48 << 20


def along_z(value, by):
    count = lax.axis_size(EXPERT)
    return lax.ppermute(value, EXPERT, [(i, ((i // 4 + by) % (count // 4)) * 4 + i % 4) for i in range(count)])


def swap(value, bits):
    return lax.ppermute(value, EXPERT, [(i, i ^ bits) for i in range(lax.axis_size(EXPERT))])


def shifted(value, axis, by):
    count = lax.axis_size(axis)
    pairs = [(i, i + by) for i in range(count) if 0 <= i + by < count]
    return lax.ppermute(value, axis, pairs)


def stage(*values):
    return lax.optimization_barrier(values)


def silu_slope(values):
    sigma = jax.nn.sigmoid(values)
    return sigma * (1.0 + values * (1.0 - sigma))


def diagonal(rows):
    row = lax.broadcasted_iota(jnp.int32, (rows, META), 0)
    return jnp.where(row == lax.broadcasted_iota(jnp.int32, (rows, META), 1), 1.0, 0.0).astype(jnp.bfloat16)


def pack_kernel(x, g, f_routes, f_gates, b_routes, b_gates, out, alone, whole, fr, fg, br, bg, sems):
    width = x.shape[1]
    pairs = (
        (f_routes, fr),
        (f_gates, fg),
        (b_routes, br),
        (b_gates, bg),
        (x, whole.at[0]),
        (g, whole.at[1]),
    )
    copies = [pltpu.make_async_copy(a, b, sems.at[i]) for i, (a, b) in enumerate(pairs)]
    for copy in copies:
        copy.start()
    for copy in copies[:4]:
        copy.wait()
    rows = []
    for routes, gates in ((br, bg), (fr, fg)):
        rows.append(routes[...].astype(jnp.float32))
        rest = gates[...]
        for _ in range(3):
            part = rest.astype(jnp.bfloat16).astype(jnp.float32)
            rows.append(part)
            rest = rest - part
    table = jnp.concatenate(rows, axis=0).astype(jnp.bfloat16)
    meta = lax.dot_general(
        table, diagonal(8 * TOP), (((0,), (0,)), ((), ())), preferred_element_type=jnp.float32
    )
    out[:, 2 * width :] = meta.astype(jnp.bfloat16)
    alone[...] = meta.astype(jnp.bfloat16)
    for i, copy in enumerate(copies[4:]):
        copy.wait()
        out[:, i * width : (i + 1) * width] = whole[i]


def pack(x, g, f_routes, f_gates, b_routes, b_gates):
    return pl.pallas_call(
        pack_kernel,
        out_shape=[
            jax.ShapeDtypeStruct((x.shape[0], columns), jnp.bfloat16) for columns in (2 * x.shape[1] + META, META)
        ],
        in_specs=[pl.BlockSpec(memory_space=pl.ANY)] * 6,
        out_specs=[VMEM] * 2,
        scratch_shapes=[pltpu.VMEM((2, *x.shape), jnp.bfloat16)]
        + [pltpu.VMEM((TOP, x.shape[0]), dtype) for dtype in (jnp.int32, jnp.float32) * 2]
        + [pltpu.SemaphoreType.DMA((6,))],
        compiler_params=pltpu.CompilerParams(vmem_limit_bytes=60 << 20),
        name="pack",
    )(x, g, f_routes.T, f_gates.T, b_routes.T, b_gates.T)


def unpack(blocks):
    meta = jnp.concatenate([b[:, b.shape[1] - META :] for b in blocks], axis=0)
    rows = lax.dot_general(
        diagonal(8 * TOP), meta, (((1,), (1,)), ((), ())), preferred_element_type=jnp.float32
    )
    both = []
    for start in (0, 4 * TOP):
        part = [rows[start + i * TOP : start + (i + 1) * TOP] for i in range(4)]
        both.append((part[0], part[1] + part[2] + part[3]))
    return both


def select_rows(ids, routes, gates, count, weights, select):
    lanes = routes.shape[1]
    tokens = lanes // FOUR
    row = lax.broadcasted_iota(jnp.int32, (2 * FOUR, lanes), 0)
    named = jnp.zeros((2 * FOUR, lanes), jnp.float32)
    gate = jnp.zeros((2 * FOUR, lanes), jnp.float32)
    for x in range(2 * FOUR):
        hit = routes == ids[x].astype(jnp.float32)
        named = jnp.where(row == x, jnp.max(jnp.where(hit, 1.0, 0.0), axis=0, keepdims=True), named)
        gate = jnp.where(row == x, jnp.sum(jnp.where(hit, gates, 0.0), axis=0, keepdims=True), gate)
    first = lax.broadcasted_iota(jnp.int32, (lanes, lanes), 0)
    second = lax.broadcasted_iota(jnp.int32, (lanes, lanes), 1)
    before = jnp.where((first < second) & (first // tokens == second // tokens), 1.0, 0.0).astype(jnp.bfloat16)
    position = jnp.dot(named.astype(jnp.bfloat16), before, preferred_element_type=jnp.float32)
    source = lax.broadcasted_iota(jnp.int32, (2 * FOUR, lanes), 1) // tokens
    slot = jnp.where(named > 0.5, position + (source * CAP).astype(jnp.float32), -1.0)
    place = lax.broadcasted_iota(jnp.int32, (PART, lanes), 0)
    early = place < PART // 2
    place = jnp.where(early, place, place - PART // 2).astype(jnp.float32)
    for a in range(count):
        match = jnp.where(early, slot[2 * a : 2 * a + 1], slot[2 * a + 1 : 2 * a + 2]) == place
        weight = jnp.where(match, jnp.where(early, gate[2 * a : 2 * a + 1], gate[2 * a + 1 : 2 * a + 2]), 0.0)
        high = weight.astype(jnp.bfloat16)
        select[a * PART : (a + 1) * PART, :] = jnp.where(match, 1.0, 0.0).astype(jnp.bfloat16)
        weights[a * PART : (a + 1) * PART, :] = high
        weights[(count + a) * PART : (count + a + 1) * PART, :] = (weight - high.astype(jnp.float32)).astype(jnp.bfloat16)


def spread(chosen, four, outs):
    tile = 512
    for i in range(outs[0].shape[1] // tile):
        at = slice(i * tile, (i + 1) * tile)
        block = jnp.concatenate([b[:, at] for b in four], axis=0)
        slots = jnp.dot(chosen, block, preferred_element_type=jnp.float32)
        for a in range(FOUR):
            outs[a][:, at] = slots[a * PART : (a + 1) * PART].astype(jnp.bfloat16)


def pick_backward_kernel(ids, b0, b1, b2, b3, p0, p1, p2, p3, weights, tables, select):
    blocks = (b0, b1, b2, b3)
    (routes, gates), (other_routes, other_gates) = unpack(blocks)
    tables[:TOP, :] = other_routes
    tables[TOP:, :] = other_gates
    select_rows(ids, routes, gates, FOUR, weights, select)
    spread(select[...], blocks, (p0, p1, p2, p3))


def pick_forward_kernel(ids, *refs):
    blocks, outs, select = refs[:10], refs[10:-1], refs[-1]
    for half in range(2):
        tables, *four = blocks[5 * half : 5 * half + 5]
        routes, gates = unpack(four)[0]
        select_rows(ids, routes, gates, 2, outs[2 * FOUR + 2 + half], select)
        select_rows(ids, tables[:TOP, :], tables[TOP:, :], FOUR, outs[2 * FOUR + half], select)
        spread(select[...], four, outs[FOUR * half : FOUR * half + FOUR])


def pick(kernel, ids, blocks, count, width, extra):
    lanes = FOUR * blocks[-1].shape[0]
    out_shape = [jax.ShapeDtypeStruct((PART, width), jnp.bfloat16)] * (FOUR * count)
    out_shape += [jax.ShapeDtypeStruct((count, lanes), dtype) for count, dtype in extra]
    outs = pl.pallas_call(
        kernel,
        out_shape=out_shape,
        in_specs=[pl.BlockSpec(memory_space=pltpu.SMEM)] + [VMEM] * len(blocks),
        out_specs=[VMEM] * len(out_shape),
        scratch_shapes=[pltpu.VMEM((FOUR * PART, lanes), jnp.bfloat16)],
        compiler_params=pltpu.CompilerParams(vmem_limit_bytes=LIMIT),
        cost_estimate=pl.CostEstimate(flops=1 << 26, bytes_accessed=1 << 20, transcendentals=0),
        name="pick",
    )(ids, *blocks)
    return list(outs[: FOUR * count]), *outs[FOUR * count :]


def pick_backward(ids, blocks, width):
    extra = [(2 * FOUR * PART, jnp.bfloat16), (2 * TOP, jnp.float32)]
    return pick(pick_backward_kernel, ids, blocks, 1, width, extra)


def pick_forward(ids, near, far, width):
    extra = [(2 * count * PART, jnp.bfloat16) for count in (FOUR, FOUR, 2, 2)]
    return pick(pick_forward_kernel, ids, (*near, *far), 2, width, extra)


def line_up(parts, j, rows):
    start = 0 if j == 0 else PART - ALIGNED
    for i, part in enumerate(parts):
        rows[i * ALIGNED : (i + 1) * ALIGNED, :] = part[start : start + ALIGNED, :]


def lay_out(results, outs):
    edge = PART // 2 // 16 * 16
    for i, out in enumerate(outs):
        at = i * ALIGNED
        out[:edge, :] = results[0, at : at + edge, :]
        low, high = results[0, at + edge : at + edge + 16, :], results[1, at : at + 16, :]
        row = lax.broadcasted_iota(jnp.int32, low.shape, 0)
        mixed = jnp.where(row < PART // 2 - edge, low.astype(jnp.float32), high.astype(jnp.float32))
        out[edge : edge + 16, :] = mixed.astype(jnp.bfloat16)
        out[edge + 16 :, :] = results[1, at + 16 : at + ALIGNED, :]


def tiles(total, tile, body):
    def step(i, _):
        body(pl.ds(pl.multiple_of(i * tile, tile), tile))
        return 0

    lax.fori_loop(0, total // tile, step, 0)


def half_rows(refs, half):
    return [ref.at[pl.ds(half * PART, PART), :] for ref in refs]


def forward_kernel(*refs):
    parts, (w_in, w_out), outs, (rows, hidden, results) = refs[:FOUR], refs[FOUR : FOUR + 2], refs[-7:-3], refs[-3:]
    for j in range(2):
        line_up(parts, j, rows)

        def into(at):
            pre = jnp.dot(rows[...], w_in[j, :, at], preferred_element_type=jnp.float32)
            hidden[:, at] = (pre * jax.nn.sigmoid(pre)).astype(jnp.bfloat16)

        def outof(at):
            out = jnp.dot(hidden[...], w_out[j, :, at], preferred_element_type=jnp.float32)
            results[j, :, at] = out.astype(jnp.bfloat16)

        tiles(hidden.shape[1], 256, into)
        tiles(rows.shape[1], 512, outof)
    lay_out(results, outs)


def backward_kernel(*refs):
    w_in, w_out, own, other, across, rows, grad_rows, hidden, results = refs[8:]
    width = rows.shape[1]
    parts = [ref.at[:, pl.ds(0, width)] for ref in refs[:8]]
    grads = [ref.at[:, pl.ds(width, width)] for ref in refs[:8]]
    outs = []
    for half in range(2):
        outs += half_rows((own, across, other), half) + half_rows((across,), 2 + half)
    across = (((1,), (1,)), ((), ()))
    for j in range(2):
        line_up(parts, j, rows)
        line_up(grads, j, grad_rows)

        def into(at):
            pre = jnp.dot(rows[...], w_in[j, :, at], preferred_element_type=jnp.float32)
            grad = lax.dot_general(grad_rows[...], w_out[j, at, :], across, preferred_element_type=jnp.float32)
            hidden[:, at] = (grad * silu_slope(pre)).astype(jnp.bfloat16)

        def outof(at):
            out = lax.dot_general(hidden[...], w_in[j, at, :], across, preferred_element_type=jnp.float32)
            results[j, :, at] = out.astype(jnp.bfloat16)

        tiles(hidden.shape[1], 256, into)
        tiles(rows.shape[1], 512, outof)
    lay_out(results, outs)


def experts(kernel, arrays, inputs, outs, weight_in, weight_out):
    width = weight_in.shape[1]
    rows = len(inputs) * ALIGNED
    return pl.pallas_call(
        kernel,
        out_shape=[jax.ShapeDtypeStruct((count * PART, width), jnp.bfloat16) for count in outs],
        in_specs=[VMEM] * (len(inputs) + 2),
        out_specs=[VMEM] * len(outs),
        scratch_shapes=[pltpu.VMEM((rows, width), jnp.bfloat16)] * arrays
        + [pltpu.VMEM((rows, weight_in.shape[2]), jnp.bfloat16), pltpu.VMEM((2, rows, width), jnp.bfloat16)],
        compiler_params=pltpu.CompilerParams(vmem_limit_bytes=LIMIT),
        cost_estimate=pl.CostEstimate(flops=1 << 28, bytes_accessed=1 << 21, transcendentals=1 << 16),
        name="experts",
    )(*inputs, weight_in, weight_out)


def gated_kernel(half, weights, p0, p1, p2, p3, s0, s1, s2, s3, every):
    for a, part in enumerate((p0, p1, p2, p3)):
        every[a * PART : (a + 1) * PART, :] = part[half * PART : (half + 1) * PART, :]
    down = (((0,), (0,)), ((), ()))
    tokens = s0.shape[0]
    tile = 512
    for i in range(every.shape[1] // tile):
        at = slice(i * tile, (i + 1) * tile)
        total = lax.dot_general(weights[: FOUR * PART, :], every[:, at], down, preferred_element_type=jnp.float32)
        total += lax.dot_general(weights[FOUR * PART :, :], every[:, at], down, preferred_element_type=jnp.float32)
        for k, out in enumerate((s0, s1, s2, s3)):
            out[:, at] = total[k * tokens : (k + 1) * tokens].astype(jnp.bfloat16)


def gated(weights, parts, half=0):
    width = parts[0].shape[1]
    tokens = weights.shape[1] // FOUR
    return pl.pallas_call(
        functools.partial(gated_kernel, half),
        out_shape=[jax.ShapeDtypeStruct((tokens, width), jnp.bfloat16)] * FOUR,
        in_specs=[VMEM] * 5,
        out_specs=[VMEM] * FOUR,
        scratch_shapes=[pltpu.VMEM((FOUR * PART, width), jnp.bfloat16)],
        compiler_params=pltpu.CompilerParams(vmem_limit_bytes=LIMIT),
        cost_estimate=pl.CostEstimate(flops=4 * 320 * 256 * width, bytes_accessed=1 << 22, transcendentals=0),
        name="gated",
    )(weights, *parts)


def gated_pair_kernel(half, weights, other_weights, own, other, across, s0, s1, s2, s3, every):
    pair = 2 * PART
    for i, (part, first) in enumerate(((own, half), (across, half), (other, half), (across, 2 + half))):
        every[i * PART : (i + 1) * PART, :] = part[first * PART : (first + 1) * PART, :]
    down = (((0,), (0,)), ((), ()))
    tokens = s0.shape[0] // 2
    tile = 512
    for i in range(every.shape[1] // tile):
        at = slice(i * tile, (i + 1) * tile)
        for n, (table, low) in enumerate(((weights, 2 * pair), (other_weights, pair))):
            rows = every[n * pair : (n + 1) * pair, at]
            total = lax.dot_general(table[:pair, :], rows, down, preferred_element_type=jnp.float32)
            total += lax.dot_general(table[low : low + pair, :], rows, down, preferred_element_type=jnp.float32)
            for k, out in enumerate((s0, s1, s2, s3)):
                out[n * tokens : (n + 1) * tokens, at] = total[k * tokens : (k + 1) * tokens].astype(jnp.bfloat16)


def gated_pair(half, weights, other_weights, parts):
    width = parts[0].shape[1]
    tokens = weights.shape[1] // FOUR
    return pl.pallas_call(
        functools.partial(gated_pair_kernel, half),
        out_shape=[jax.ShapeDtypeStruct((2 * tokens, width), jnp.bfloat16)] * FOUR,
        in_specs=[VMEM] * 5,
        out_specs=[VMEM] * FOUR,
        scratch_shapes=[pltpu.VMEM((FOUR * PART, width), jnp.bfloat16)],
        compiler_params=pltpu.CompilerParams(vmem_limit_bytes=LIMIT),
        cost_estimate=pl.CostEstimate(flops=4 * 320 * 256 * width, bytes_accessed=1 << 22, transcendentals=0),
        name="gated_pair",
    )(weights, other_weights, *parts)


def hop(up, down):
    return along_z(up, 1), along_z(down, -1)


def far_hop(up, down):
    half = up.shape[0] // 2
    return along_z(up[:half], 1), along_z(down[half:], -1)


def added(one, two):
    return (one.astype(jnp.float32) + two.astype(jnp.float32)).astype(jnp.bfloat16)


def turn_back(last):
    half = last.shape[0] // 2
    return along_z(last[half:], 1), along_z(last[:half], -1)


def add_halves(up, down, pair):
    half = up.shape[0] // 2
    up = jnp.concatenate([up[:half], added(up[half:], pair[0])], axis=0)
    down = jnp.concatenate([added(down[:half], pair[1]), down[half:]], axis=0)
    return up, down


def finished(base, own, pair):
    total = base.astype(jnp.float32) + own.astype(jnp.float32)
    return (total + pair[0].astype(jnp.float32) + pair[1].astype(jnp.float32)).astype(jnp.bfloat16)


def exchange(parts):
    return [parts[0]] + [swap(parts[a], a) for a in (1, 2, 3)]


def per_device(
    fwd_input, fwd_routes, fwd_gates, bwd_input, bwd_grad, bwd_routes, bwd_gates, w_in, w_out
):
    weight_in, weight_out = w_in[0], w_out[0]
    f_own = fwd_input[0]
    width = f_own.shape[1]
    me = lax.axis_index(EXPERT)
    ids = jnp.stack([2 * (me ^ a) + j for a in range(4) for j in range(2)]).astype(jnp.int32)
    b_own, meta = pack(bwd_input[0], bwd_grad[0], fwd_routes[0], fwd_gates[0], bwd_routes[0], bwd_gates[0])

    b1 = hop(b_own, b_own)
    meta = swap(meta, 2)
    b1, meta = stage(b1, meta)
    b2 = hop(*b1)
    f_own = jnp.concatenate([f_own, meta], axis=1)
    b2, f_own = stage(b2, f_own)
    b_parts1, b_weights1, near = pick_backward(ids, (*b1, *b2), 2 * width)
    b2, b_parts1, f_own = stage(b2, b_parts1, f_own)

    b_got1 = exchange(b_parts1)
    b3 = hop(*b2)
    b4 = far_hop(*b3)
    f1 = hop(f_own, f_own)
    b_got1, b3, b4, f1 = stage(b_got1, b3, b4, f1)
    b_parts2, b_weights2, far = pick_backward(ids, (b_own, *b3, jnp.concatenate(b4, axis=0)), 2 * width)
    b_parts2, f1 = stage(b_parts2, f1)

    b_got2 = exchange(b_parts2)
    f2 = hop(*f1)
    f3 = hop(*f2)
    f4 = far_hop(*f3)
    b_got2, f2, f3, f4 = stage(b_got2, f2, f3, f4)
    f_parts, f_weights1, f_weights2, b_others1, b_others2 = pick_forward(
        ids, (near, *f1, *f2), (far, f_own, *f3, jnp.concatenate(f4, axis=0)), width
    )
    f_parts, b_got1, b_got2 = stage(f_parts, b_got1, b_got2)

    f_got2 = exchange(f_parts[4:])
    b_out = experts(backward_kernel, 2, b_got1 + b_got2, (2, 2, 4), weight_in, weight_out)
    f_got2, b_out, f_parts1 = stage(f_got2, b_out, f_parts[:4])

    f_got1 = exchange(f_parts1)
    f_out2 = experts(forward_kernel, 1, f_got2, (1,) * 4, weight_in, weight_out)
    b_out = [b_out[0], b_out[1], swap(b_out[2], 1)]
    b_sums2 = gated_pair(1, b_weights2, b_others2, b_out)
    b_pair = turn_back(b_sums2[3])
    f_got1, f_out2, b_out, b_sums2, b_pair = stage(f_got1, f_out2, b_out, b_sums2, b_pair)

    f_back2 = exchange(f_out2)
    b_pair = hop(*add_halves(b_sums2[2], b_sums2[1], b_pair))
    f_out1 = experts(forward_kernel, 1, f_got1, (1,) * 4, weight_in, weight_out)
    b_sums1 = gated_pair(0, b_weights1, b_others1, b_out)
    f_sums2 = gated(f_weights2, f_back2)
    b_pair, f_out1, b_sums1, f_sums2 = stage(b_pair, f_out1, b_sums1, f_sums2)

    f_back1 = exchange(f_out1)
    rows = b_sums1[0].shape[0]
    half = f_sums2[3].shape[0] // 2
    pair = hop(
        jnp.concatenate([added(b_sums1[3], b_pair[0]), f_sums2[3][half:]], axis=0),
        jnp.concatenate([added(b_sums1[2], b_pair[1]), f_sums2[3][:half]], axis=0),
    )
    f_sums1 = gated(f_weights1, f_back1)
    pair, f_sums1 = stage(pair, f_sums1)

    f_pair = add_halves(f_sums2[2], f_sums2[1], (pair[0][rows:], pair[1][rows:]))
    pair = hop(
        jnp.concatenate([added(b_sums1[1], pair[0][:rows]), f_pair[0]], axis=0),
        jnp.concatenate([added(b_sums1[0], pair[1][:rows]), f_pair[1]], axis=0),
    )
    pair = stage(*pair)

    f_pair = hop(added(f_sums1[3], pair[0][rows:]), added(f_sums1[2], pair[1][rows:]))
    b_sum = b_sums2[0].astype(jnp.float32) + pair[0][:rows].astype(jnp.float32) + pair[1][:rows].astype(jnp.float32)
    b_other = swap(b_sum[rows // 2 :].astype(jnp.bfloat16), 2)
    f_pair, b_other = stage(f_pair, b_other)
    b_sum = b_sum[: rows // 2] + bwd_grad[0].astype(jnp.float32) + b_other.astype(jnp.float32)
    next_cotangent = shifted(b_sum.astype(jnp.bfloat16)[None], "pipe", -1)
    f_pair = hop(added(f_sums1[1], f_pair[0]), added(f_sums1[0], f_pair[1]))
    next_forward = shifted(finished(fwd_input[0], f_sums2[0], f_pair)[None], "pipe", 1)
    return (next_forward, next_cotangent)


def solution(mesh):
    rows = P("pipe", "expert", None)
    weights = P("pipe", "expert", None, None)
    return jax.shard_map(
        per_device,
        mesh=mesh,
        in_specs=(rows,) * 7 + (weights,) * 2,
        out_specs=(rows, rows),
        check_vma=False,
    )
```

```python
import functools

import jax
import jax.numpy as jnp
from jax import lax
from jax.experimental import pallas as pl
from jax.experimental.pallas import tpu as pltpu
from jax.sharding import PartitionSpec as P

TOP = 8
CAP = 10
EXPERT = "expert"
NEAR = (1, -1, 2, -2)
FAR = (0, 3, -3, 4)
FOUR = 4
PART = 2 * FOUR * CAP
ALIGNED = 48
META = 128
VMEM = pl.BlockSpec(memory_space=pltpu.VMEM)
LIMIT = 48 << 20


def along_z(value, by):
    count = lax.axis_size(EXPERT)
    return lax.ppermute(value, EXPERT, [(i, ((i // 4 + by) % (count // 4)) * 4 + i % 4) for i in range(count)])


def swap(value, bits):
    return lax.ppermute(value, EXPERT, [(i, i ^ bits) for i in range(lax.axis_size(EXPERT))])


def shifted(value, axis, by):
    count = lax.axis_size(axis)
    pairs = [(i, i + by) for i in range(count) if 0 <= i + by < count]
    return lax.ppermute(value, axis, pairs)


def stage(*values):
    return lax.optimization_barrier(values)


def silu_slope(values):
    sigma = jax.nn.sigmoid(values)
    return sigma * (1.0 + values * (1.0 - sigma))


def diagonal(rows):
    row = lax.broadcasted_iota(jnp.int32, (rows, META), 0)
    return jnp.where(row == lax.broadcasted_iota(jnp.int32, (rows, META), 1), 1.0, 0.0).astype(jnp.bfloat16)


def pack_kernel(x, g, f_routes, f_gates, b_routes, b_gates, out, alone, whole, fr, fg, br, bg, sems):
    width = x.shape[1]
    pairs = (
        (f_routes, fr),
        (f_gates, fg),
        (b_routes, br),
        (b_gates, bg),
        (x, whole.at[0]),
        (g, whole.at[1]),
    )
    copies = [pltpu.make_async_copy(a, b, sems.at[i]) for i, (a, b) in enumerate(pairs)]
    for copy in copies:
        copy.start()
    for copy in copies[:4]:
        copy.wait()
    rows = []
    for routes, gates in ((br, bg), (fr, fg)):
        rows.append(routes[...].astype(jnp.float32))
        rest = gates[...]
        for _ in range(3):
            part = rest.astype(jnp.bfloat16).astype(jnp.float32)
            rows.append(part)
            rest = rest - part
    table = jnp.concatenate(rows, axis=0).astype(jnp.bfloat16)
    meta = lax.dot_general(
        table, diagonal(8 * TOP), (((0,), (0,)), ((), ())), preferred_element_type=jnp.float32
    )
    out[:, 2 * width :] = meta.astype(jnp.bfloat16)
    alone[...] = meta.astype(jnp.bfloat16)
    for i, copy in enumerate(copies[4:]):
        copy.wait()
        out[:, i * width : (i + 1) * width] = whole[i]


def pack(x, g, f_routes, f_gates, b_routes, b_gates):
    return pl.pallas_call(
        pack_kernel,
        out_shape=[
            jax.ShapeDtypeStruct((x.shape[0], columns), jnp.bfloat16) for columns in (2 * x.shape[1] + META, META)
        ],
        in_specs=[pl.BlockSpec(memory_space=pl.ANY)] * 6,
        out_specs=[VMEM] * 2,
        scratch_shapes=[pltpu.VMEM((2, *x.shape), jnp.bfloat16)]
        + [pltpu.VMEM((TOP, x.shape[0]), dtype) for dtype in (jnp.int32, jnp.float32) * 2]
        + [pltpu.SemaphoreType.DMA((6,))],
        compiler_params=pltpu.CompilerParams(vmem_limit_bytes=60 << 20),
        name="pack",
    )(x, g, f_routes.T, f_gates.T, b_routes.T, b_gates.T)


def unpack(blocks):
    meta = jnp.concatenate([b[:, b.shape[1] - META :] for b in blocks], axis=0)
    rows = lax.dot_general(
        diagonal(8 * TOP), meta, (((1,), (1,)), ((), ())), preferred_element_type=jnp.float32
    )
    both = []
    for start in (0, 4 * TOP):
        part = [rows[start + i * TOP : start + (i + 1) * TOP] for i in range(4)]
        both.append((part[0], part[1] + part[2] + part[3]))
    return both


def select_rows(ids, routes, gates, count, weights, select):
    lanes = routes.shape[1]
    tokens = lanes // FOUR
    row = lax.broadcasted_iota(jnp.int32, (2 * FOUR, lanes), 0)
    named = jnp.zeros((2 * FOUR, lanes), jnp.float32)
    gate = jnp.zeros((2 * FOUR, lanes), jnp.float32)
    for x in range(2 * FOUR):
        hit = routes == ids[x].astype(jnp.float32)
        named = jnp.where(row == x, jnp.max(jnp.where(hit, 1.0, 0.0), axis=0, keepdims=True), named)
        gate = jnp.where(row == x, jnp.sum(jnp.where(hit, gates, 0.0), axis=0, keepdims=True), gate)
    first = lax.broadcasted_iota(jnp.int32, (lanes, lanes), 0)
    second = lax.broadcasted_iota(jnp.int32, (lanes, lanes), 1)
    before = jnp.where((first < second) & (first // tokens == second // tokens), 1.0, 0.0).astype(jnp.bfloat16)
    position = jnp.dot(named.astype(jnp.bfloat16), before, preferred_element_type=jnp.float32)
    source = lax.broadcasted_iota(jnp.int32, (2 * FOUR, lanes), 1) // tokens
    slot = jnp.where(named > 0.5, position + (source * CAP).astype(jnp.float32), -1.0)
    place = lax.broadcasted_iota(jnp.int32, (PART, lanes), 0)
    early = place < PART // 2
    place = jnp.where(early, place, place - PART // 2).astype(jnp.float32)
    for a in range(count):
        match = jnp.where(early, slot[2 * a : 2 * a + 1], slot[2 * a + 1 : 2 * a + 2]) == place
        weight = jnp.where(match, jnp.where(early, gate[2 * a : 2 * a + 1], gate[2 * a + 1 : 2 * a + 2]), 0.0)
        high = weight.astype(jnp.bfloat16)
        select[a * PART : (a + 1) * PART, :] = jnp.where(match, 1.0, 0.0).astype(jnp.bfloat16)
        weights[a * PART : (a + 1) * PART, :] = high
        weights[(count + a) * PART : (count + a + 1) * PART, :] = (weight - high.astype(jnp.float32)).astype(jnp.bfloat16)


def spread(chosen, four, outs):
    tile = 512
    for i in range(outs[0].shape[1] // tile):
        at = slice(i * tile, (i + 1) * tile)
        block = jnp.concatenate([b[:, at] for b in four], axis=0)
        slots = jnp.dot(chosen, block, preferred_element_type=jnp.float32)
        for a in range(FOUR):
            outs[a][:, at] = slots[a * PART : (a + 1) * PART].astype(jnp.bfloat16)


def pick_backward_kernel(ids, b0, b1, b2, b3, p0, p1, p2, p3, weights, tables, select):
    blocks = (b0, b1, b2, b3)
    (routes, gates), (other_routes, other_gates) = unpack(blocks)
    tables[:TOP, :] = other_routes
    tables[TOP:, :] = other_gates
    select_rows(ids, routes, gates, FOUR, weights, select)
    spread(select[...], blocks, (p0, p1, p2, p3))


def pick_forward_kernel(ids, *refs):
    blocks, outs, select = refs[:10], refs[10:-1], refs[-1]
    for half in range(2):
        tables, *four = blocks[5 * half : 5 * half + 5]
        routes, gates = unpack(four)[0]
        select_rows(ids, routes, gates, 2, outs[2 * FOUR + 2 + half], select)
        select_rows(ids, tables[:TOP, :], tables[TOP:, :], FOUR, outs[2 * FOUR + half], select)
        spread(select[...], four, outs[FOUR * half : FOUR * half + FOUR])


def pick(kernel, ids, blocks, count, width, extra):
    lanes = FOUR * blocks[-1].shape[0]
    out_shape = [jax.ShapeDtypeStruct((PART, width), jnp.bfloat16)] * (FOUR * count)
    out_shape += [jax.ShapeDtypeStruct((count, lanes), dtype) for count, dtype in extra]
    outs = pl.pallas_call(
        kernel,
        out_shape=out_shape,
        in_specs=[pl.BlockSpec(memory_space=pltpu.SMEM)] + [VMEM] * len(blocks),
        out_specs=[VMEM] * len(out_shape),
        scratch_shapes=[pltpu.VMEM((FOUR * PART, lanes), jnp.bfloat16)],
        compiler_params=pltpu.CompilerParams(vmem_limit_bytes=LIMIT),
        cost_estimate=pl.CostEstimate(flops=1 << 26, bytes_accessed=1 << 20, transcendentals=0),
        name="pick",
    )(ids, *blocks)
    return list(outs[: FOUR * count]), *outs[FOUR * count :]


def pick_backward(ids, blocks, width):
    extra = [(2 * FOUR * PART, jnp.bfloat16), (2 * TOP, jnp.float32)]
    return pick(pick_backward_kernel, ids, blocks, 1, width, extra)


def pick_forward(ids, near, far, width):
    extra = [(2 * count * PART, jnp.bfloat16) for count in (FOUR, FOUR, 2, 2)]
    return pick(pick_forward_kernel, ids, (*near, *far), 2, width, extra)


def line_up(parts, j, rows):
    start = 0 if j == 0 else PART - ALIGNED
    for i, part in enumerate(parts):
        rows[i * ALIGNED : (i + 1) * ALIGNED, :] = part[start : start + ALIGNED, :]


def lay_out(results, outs):
    edge = PART // 2 // 16 * 16
    for i, out in enumerate(outs):
        at = i * ALIGNED
        out[:edge, :] = results[0, at : at + edge, :]
        low, high = results[0, at + edge : at + edge + 16, :], results[1, at : at + 16, :]
        row = lax.broadcasted_iota(jnp.int32, low.shape, 0)
        mixed = jnp.where(row < PART // 2 - edge, low.astype(jnp.float32), high.astype(jnp.float32))
        out[edge : edge + 16, :] = mixed.astype(jnp.bfloat16)
        out[edge + 16 :, :] = results[1, at + 16 : at + ALIGNED, :]


def tiles(total, tile, body):
    def step(i, _):
        body(pl.ds(pl.multiple_of(i * tile, tile), tile))
        return 0

    lax.fori_loop(0, total // tile, step, 0)


def half_rows(refs, half):
    return [ref.at[pl.ds(half * PART, PART), :] for ref in refs]


def forward_kernel(*refs):
    parts, (w_in, w_out), outs, (rows, hidden, results) = refs[:FOUR], refs[FOUR : FOUR + 2], refs[-7:-3], refs[-3:]
    for j in range(2):
        line_up(parts, j, rows)

        def into(at):
            pre = jnp.dot(rows[...], w_in[j, :, at], preferred_element_type=jnp.float32)
            hidden[:, at] = (pre * jax.nn.sigmoid(pre)).astype(jnp.bfloat16)

        def outof(at):
            out = jnp.dot(hidden[...], w_out[j, :, at], preferred_element_type=jnp.float32)
            results[j, :, at] = out.astype(jnp.bfloat16)

        tiles(hidden.shape[1], 256, into)
        tiles(rows.shape[1], 512, outof)
    lay_out(results, outs)


def backward_kernel(*refs):
    w_in, w_out, own, other, across, rows, grad_rows, hidden, results = refs[8:]
    width = rows.shape[1]
    parts = [ref.at[:, pl.ds(0, width)] for ref in refs[:8]]
    grads = [ref.at[:, pl.ds(width, width)] for ref in refs[:8]]
    outs = []
    for half in range(2):
        outs += half_rows((own, across, other), half) + half_rows((across,), 2 + half)
    across = (((1,), (1,)), ((), ()))
    for j in range(2):
        line_up(parts, j, rows)
        line_up(grads, j, grad_rows)

        def into(at):
            pre = jnp.dot(rows[...], w_in[j, :, at], preferred_element_type=jnp.float32)
            grad = lax.dot_general(grad_rows[...], w_out[j, at, :], across, preferred_element_type=jnp.float32)
            hidden[:, at] = (grad * silu_slope(pre)).astype(jnp.bfloat16)

        def outof(at):
            out = lax.dot_general(hidden[...], w_in[j, at, :], across, preferred_element_type=jnp.float32)
            results[j, :, at] = out.astype(jnp.bfloat16)

        tiles(hidden.shape[1], 256, into)
        tiles(rows.shape[1], 512, outof)
    lay_out(results, outs)


def experts(kernel, arrays, inputs, outs, weight_in, weight_out):
    width = weight_in.shape[1]
    rows = len(inputs) * ALIGNED
    return pl.pallas_call(
        kernel,
        out_shape=[jax.ShapeDtypeStruct((count * PART, width), jnp.bfloat16) for count in outs],
        in_specs=[VMEM] * (len(inputs) + 2),
        out_specs=[VMEM] * len(outs),
        scratch_shapes=[pltpu.VMEM((rows, width), jnp.bfloat16)] * arrays
        + [pltpu.VMEM((rows, weight_in.shape[2]), jnp.bfloat16), pltpu.VMEM((2, rows, width), jnp.bfloat16)],
        compiler_params=pltpu.CompilerParams(vmem_limit_bytes=LIMIT),
        cost_estimate=pl.CostEstimate(flops=1 << 28, bytes_accessed=1 << 21, transcendentals=1 << 16),
        name="experts",
    )(*inputs, weight_in, weight_out)


def gated_kernel(half, weights, p0, p1, p2, p3, s0, s1, s2, s3, every):
    for a, part in enumerate((p0, p1, p2, p3)):
        every[a * PART : (a + 1) * PART, :] = part[half * PART : (half + 1) * PART, :]
    down = (((0,), (0,)), ((), ()))
    tokens = s0.shape[0]
    tile = 512
    for i in range(every.shape[1] // tile):
        at = slice(i * tile, (i + 1) * tile)
        total = lax.dot_general(weights[: FOUR * PART, :], every[:, at], down, preferred_element_type=jnp.float32)
        total += lax.dot_general(weights[FOUR * PART :, :], every[:, at], down, preferred_element_type=jnp.float32)
        for k, out in enumerate((s0, s1, s2, s3)):
            out[:, at] = total[k * tokens : (k + 1) * tokens].astype(jnp.bfloat16)


def gated(weights, parts, half=0):
    width = parts[0].shape[1]
    tokens = weights.shape[1] // FOUR
    return pl.pallas_call(
        functools.partial(gated_kernel, half),
        out_shape=[jax.ShapeDtypeStruct((tokens, width), jnp.bfloat16)] * FOUR,
        in_specs=[VMEM] * 5,
        out_specs=[VMEM] * FOUR,
        scratch_shapes=[pltpu.VMEM((FOUR * PART, width), jnp.bfloat16)],
        compiler_params=pltpu.CompilerParams(vmem_limit_bytes=LIMIT),
        cost_estimate=pl.CostEstimate(flops=1 << 34, bytes_accessed=1 << 22, transcendentals=0),
        name="gated",
    )(weights, *parts)


def gated_pair_kernel(half, weights, other_weights, own, other, across, s0, s1, s2, s3, every):
    pair = 2 * PART
    for i, (part, first) in enumerate(((own, half), (across, half), (other, half), (across, 2 + half))):
        every[i * PART : (i + 1) * PART, :] = part[first * PART : (first + 1) * PART, :]
    down = (((0,), (0,)), ((), ()))
    tokens = s0.shape[0] // 2
    tile = 512
    for i in range(every.shape[1] // tile):
        at = slice(i * tile, (i + 1) * tile)
        for n, (table, low) in enumerate(((weights, 2 * pair), (other_weights, pair))):
            rows = every[n * pair : (n + 1) * pair, at]
            total = lax.dot_general(table[:pair, :], rows, down, preferred_element_type=jnp.float32)
            total += lax.dot_general(table[low : low + pair, :], rows, down, preferred_element_type=jnp.float32)
            for k, out in enumerate((s0, s1, s2, s3)):
                out[n * tokens : (n + 1) * tokens, at] = total[k * tokens : (k + 1) * tokens].astype(jnp.bfloat16)


def gated_pair(half, weights, other_weights, parts):
    width = parts[0].shape[1]
    tokens = weights.shape[1] // FOUR
    return pl.pallas_call(
        functools.partial(gated_pair_kernel, half),
        out_shape=[jax.ShapeDtypeStruct((2 * tokens, width), jnp.bfloat16)] * FOUR,
        in_specs=[VMEM] * 5,
        out_specs=[VMEM] * FOUR,
        scratch_shapes=[pltpu.VMEM((FOUR * PART, width), jnp.bfloat16)],
        compiler_params=pltpu.CompilerParams(vmem_limit_bytes=LIMIT),
        cost_estimate=pl.CostEstimate(flops=4 * 320 * 256 * width, bytes_accessed=1 << 22, transcendentals=0),
        name="gated_pair",
    )(weights, other_weights, *parts)


def hop(up, down):
    return along_z(up, 1), along_z(down, -1)


def far_hop(up, down):
    half = up.shape[0] // 2
    return along_z(up[:half], 1), along_z(down[half:], -1)


def added(one, two):
    return (one.astype(jnp.float32) + two.astype(jnp.float32)).astype(jnp.bfloat16)


def turn_back(last):
    half = last.shape[0] // 2
    return along_z(last[half:], 1), along_z(last[:half], -1)


def add_halves(up, down, pair):
    half = up.shape[0] // 2
    up = jnp.concatenate([up[:half], added(up[half:], pair[0])], axis=0)
    down = jnp.concatenate([added(down[:half], pair[1]), down[half:]], axis=0)
    return up, down


def finished(base, own, others):
    total = base.astype(jnp.float32) + own.astype(jnp.float32)
    for other in others:
        total += other.astype(jnp.float32)
    return total.astype(jnp.bfloat16)


def exchange(parts):
    return [parts[0]] + [swap(parts[a], a) for a in (1, 2, 3)]


def per_device(
    fwd_input, fwd_routes, fwd_gates, bwd_input, bwd_grad, bwd_routes, bwd_gates, w_in, w_out
):
    weight_in, weight_out = w_in[0], w_out[0]
    f_own = fwd_input[0]
    width = f_own.shape[1]
    me = lax.axis_index(EXPERT)
    ids = jnp.stack([2 * (me ^ a) + j for a in range(4) for j in range(2)]).astype(jnp.int32)
    b_own, meta = pack(bwd_input[0], bwd_grad[0], fwd_routes[0], fwd_gates[0], bwd_routes[0], bwd_gates[0])

    b1 = hop(b_own, b_own)
    meta = swap(meta, 2)
    b1, meta = stage(b1, meta)
    b2 = hop(*b1)
    f_own = jnp.concatenate([f_own, meta], axis=1)
    b2, f_own = stage(b2, f_own)
    b_parts1, b_weights1, near = pick_backward(ids, (*b1, *b2), 2 * width)
    b2, b_parts1, f_own = stage(b2, b_parts1, f_own)

    b_got1 = exchange(b_parts1)
    b3 = hop(*b2)
    b4 = far_hop(*b3)
    f1 = hop(f_own, f_own)
    b_got1, b3, b4, f1 = stage(b_got1, b3, b4, f1)
    b_parts2, b_weights2, far = pick_backward(ids, (b_own, *b3, jnp.concatenate(b4, axis=0)), 2 * width)
    b_parts2, f1 = stage(b_parts2, f1)

    b_got2 = exchange(b_parts2)
    f2 = hop(*f1)
    f3 = hop(*f2)
    f4 = far_hop(*f3)
    b_got2, f2, f3, f4 = stage(b_got2, f2, f3, f4)
    f_parts, f_weights1, f_weights2, b_others1, b_others2 = pick_forward(
        ids, (near, *f1, *f2), (far, f_own, *f3, jnp.concatenate(f4, axis=0)), width
    )
    f_parts, b_got1, b_got2 = stage(f_parts, b_got1, b_got2)

    f_got2 = exchange(f_parts[4:])
    b_out = experts(backward_kernel, 2, b_got1 + b_got2, (2, 2, 4), weight_in, weight_out)
    f_got2, b_out, f_parts1 = stage(f_got2, b_out, f_parts[:4])

    f_got1 = exchange(f_parts1)
    f_out2 = experts(forward_kernel, 1, f_got2, (1,) * 4, weight_in, weight_out)
    b_out = [b_out[0], b_out[1], swap(b_out[2], 1)]
    b_sums2 = gated_pair(1, b_weights2, b_others2, b_out)
    b_pair = turn_back(b_sums2[3])
    f_got1, f_out2, b_out, b_sums2, b_pair = stage(f_got1, f_out2, b_out, b_sums2, b_pair)

    f_back2 = exchange(f_out2)
    b_pair = hop(*add_halves(b_sums2[2], b_sums2[1], b_pair))
    f_out1 = experts(forward_kernel, 1, f_got1, (1,) * 4, weight_in, weight_out)
    b_sums1 = gated_pair(0, b_weights1, b_others1, b_out)
    f_sums2 = gated(f_weights2, f_back2)
    b_pair, f_out1, b_sums1, f_sums2 = stage(b_pair, f_out1, b_sums1, f_sums2)

    f_back1 = exchange(f_out1)
    rows = b_sums1[0].shape[0]
    half = f_sums2[3].shape[0] // 2
    pair = hop(
        jnp.concatenate([added(b_sums1[3], b_pair[0]), f_sums2[3][half:]], axis=0),
        jnp.concatenate([added(b_sums1[2], b_pair[1]), f_sums2[3][:half]], axis=0),
    )
    f_sums1 = gated(f_weights1, f_back1)
    pair, f_sums1 = stage(pair, f_sums1)

    half = rows // 2
    f_pair = add_halves(f_sums2[2], f_sums2[1], (pair[0][rows:], pair[1][rows:]))
    b_pair = added(b_sums1[1], pair[0][:rows]), added(b_sums1[0], pair[1][:rows])
    pair = hop(*(jnp.concatenate([b[half:], f], axis=0) for b, f in zip(b_pair, f_pair)))
    pair, b_pair = stage(pair, [b[:half] for b in b_pair])

    b_other = finished(b_sums2[0][half:], pair[0][:half], (pair[1][:half],))
    b_other = swap(b_other, 2)
    f_pair = added(f_sums1[3], pair[0][half:]), added(f_sums1[2], pair[1][half:])
    pair = hop(*(jnp.concatenate([b, f], axis=0) for b, f in zip(b_pair, f_pair)))
    pair, b_other = stage(pair, b_other)

    f_pair = hop(added(f_sums1[1], pair[0][half:]), added(f_sums1[0], pair[1][half:]))
    bwd_out = finished(bwd_grad[0], b_sums2[0][:half], (pair[0][:half], pair[1][:half], b_other))
    next_cotangent = shifted(bwd_out[None], "pipe", -1)
    next_forward = shifted(finished(fwd_input[0], f_sums2[0], f_pair)[None], "pipe", 1)
    return (next_forward, next_cotangent)


def solution(mesh):
    rows = P("pipe", "expert", None)
    weights = P("pipe", "expert", None, None)
    return jax.shard_map(
        per_device,
        mesh=mesh,
        in_specs=(rows,) * 7 + (weights,) * 2,
        out_specs=(rows, rows),
        check_vma=False,
    )
```

```python
import functools

import jax
import jax.numpy as jnp
from jax import lax
from jax.experimental import pallas as pl
from jax.experimental.pallas import tpu as pltpu
from jax.sharding import PartitionSpec as P

TOP = 8
CAP = 10
EXPERT = "expert"
NEAR = (1, -1, 2, -2)
FAR = (0, 3, -3, 4)
FOUR = 4
PART = 2 * FOUR * CAP
ALIGNED = 48
META = 128
VMEM = pl.BlockSpec(memory_space=pltpu.VMEM)
LIMIT = 48 << 20


def along_z(value, by):
    count = lax.axis_size(EXPERT)
    return lax.ppermute(value, EXPERT, [(i, ((i // 4 + by) % (count // 4)) * 4 + i % 4) for i in range(count)])


def swap(value, bits):
    return lax.ppermute(value, EXPERT, [(i, i ^ bits) for i in range(lax.axis_size(EXPERT))])


def shifted(value, axis, by):
    count = lax.axis_size(axis)
    pairs = [(i, i + by) for i in range(count) if 0 <= i + by < count]
    return lax.ppermute(value, axis, pairs)


def stage(*values):
    return lax.optimization_barrier(values)


def silu_slope(values):
    sigma = jax.nn.sigmoid(values)
    return sigma * (1.0 + values * (1.0 - sigma))


def diagonal(rows):
    row = lax.broadcasted_iota(jnp.int32, (rows, META), 0)
    return jnp.where(row == lax.broadcasted_iota(jnp.int32, (rows, META), 1), 1.0, 0.0).astype(jnp.bfloat16)


def pack_kernel(x, g, f_routes, f_gates, b_routes, b_gates, out, alone, whole, fr, fg, br, bg, sems):
    width = x.shape[1]
    pairs = (
        (f_routes, fr),
        (f_gates, fg),
        (b_routes, br),
        (b_gates, bg),
        (x, whole.at[0]),
        (g, whole.at[1]),
    )
    copies = [pltpu.make_async_copy(a, b, sems.at[i]) for i, (a, b) in enumerate(pairs)]
    for copy in copies:
        copy.start()
    for copy in copies[:4]:
        copy.wait()
    rows = []
    for routes, gates in ((br, bg), (fr, fg)):
        rows.append(routes[...].astype(jnp.float32))
        rest = gates[...]
        for _ in range(3):
            part = rest.astype(jnp.bfloat16).astype(jnp.float32)
            rows.append(part)
            rest = rest - part
    table = jnp.concatenate(rows, axis=0).astype(jnp.bfloat16)
    meta = lax.dot_general(
        table, diagonal(8 * TOP), (((0,), (0,)), ((), ())), preferred_element_type=jnp.float32
    )
    out[:, 2 * width :] = meta.astype(jnp.bfloat16)
    alone[...] = meta.astype(jnp.bfloat16)
    for i, copy in enumerate(copies[4:]):
        copy.wait()
        out[:, i * width : (i + 1) * width] = whole[i]


def pack(x, g, f_routes, f_gates, b_routes, b_gates):
    return pl.pallas_call(
        pack_kernel,
        out_shape=[
            jax.ShapeDtypeStruct((x.shape[0], columns), jnp.bfloat16) for columns in (2 * x.shape[1] + META, META)
        ],
        in_specs=[pl.BlockSpec(memory_space=pl.ANY)] * 6,
        out_specs=[VMEM] * 2,
        scratch_shapes=[pltpu.VMEM((2, *x.shape), jnp.bfloat16)]
        + [pltpu.VMEM((TOP, x.shape[0]), dtype) for dtype in (jnp.int32, jnp.float32) * 2]
        + [pltpu.SemaphoreType.DMA((6,))],
        compiler_params=pltpu.CompilerParams(vmem_limit_bytes=60 << 20),
        name="pack",
    )(x, g, f_routes.T, f_gates.T, b_routes.T, b_gates.T)


def unpack(blocks):
    meta = jnp.concatenate([b[:, b.shape[1] - META :] for b in blocks], axis=0)
    rows = lax.dot_general(
        diagonal(8 * TOP), meta, (((1,), (1,)), ((), ())), preferred_element_type=jnp.float32
    )
    both = []
    for start in (0, 4 * TOP):
        part = [rows[start + i * TOP : start + (i + 1) * TOP] for i in range(4)]
        both.append((part[0], part[1] + part[2] + part[3]))
    return both


def select_rows(ids, routes, gates, count, weights, select):
    lanes = routes.shape[1]
    tokens = lanes // FOUR
    row = lax.broadcasted_iota(jnp.int32, (2 * FOUR, lanes), 0)
    named = jnp.zeros((2 * FOUR, lanes), jnp.float32)
    gate = jnp.zeros((2 * FOUR, lanes), jnp.float32)
    for x in range(2 * FOUR):
        hit = routes == ids[x].astype(jnp.float32)
        named = jnp.where(row == x, jnp.max(jnp.where(hit, 1.0, 0.0), axis=0, keepdims=True), named)
        gate = jnp.where(row == x, jnp.sum(jnp.where(hit, gates, 0.0), axis=0, keepdims=True), gate)
    first = lax.broadcasted_iota(jnp.int32, (lanes, lanes), 0)
    second = lax.broadcasted_iota(jnp.int32, (lanes, lanes), 1)
    before = jnp.where((first < second) & (first // tokens == second // tokens), 1.0, 0.0).astype(jnp.bfloat16)
    position = jnp.dot(named.astype(jnp.bfloat16), before, preferred_element_type=jnp.float32)
    source = lax.broadcasted_iota(jnp.int32, (2 * FOUR, lanes), 1) // tokens
    slot = jnp.where(named > 0.5, position + (source * CAP).astype(jnp.float32), -1.0)
    place = lax.broadcasted_iota(jnp.int32, (PART, lanes), 0)
    early = place < PART // 2
    place = jnp.where(early, place, place - PART // 2).astype(jnp.float32)
    for a in range(count):
        match = jnp.where(early, slot[2 * a : 2 * a + 1], slot[2 * a + 1 : 2 * a + 2]) == place
        weight = jnp.where(match, jnp.where(early, gate[2 * a : 2 * a + 1], gate[2 * a + 1 : 2 * a + 2]), 0.0)
        high = weight.astype(jnp.bfloat16)
        select[a * PART : (a + 1) * PART, :] = jnp.where(match, 1.0, 0.0).astype(jnp.bfloat16)
        weights[a * PART : (a + 1) * PART, :] = high
        weights[(count + a) * PART : (count + a + 1) * PART, :] = (weight - high.astype(jnp.float32)).astype(jnp.bfloat16)


def spread(chosen, four, outs):
    tile = 512
    for i in range(outs[0].shape[1] // tile):
        at = slice(i * tile, (i + 1) * tile)
        block = jnp.concatenate([b[:, at] for b in four], axis=0)
        slots = jnp.dot(chosen, block, preferred_element_type=jnp.float32)
        for a in range(FOUR):
            outs[a][:, at] = slots[a * PART : (a + 1) * PART].astype(jnp.bfloat16)


def pick_backward_kernel(ids, b0, b1, b2, b3, p0, p1, p2, p3, weights, tables, select):
    blocks = (b0, b1, b2, b3)
    (routes, gates), (other_routes, other_gates) = unpack(blocks)
    tables[:TOP, :] = other_routes
    tables[TOP:, :] = other_gates
    select_rows(ids, routes, gates, FOUR, weights, select)
    spread(select[...], blocks, (p0, p1, p2, p3))


def pick_forward_kernel(ids, *refs):
    blocks, outs, select = refs[:10], refs[10:-1], refs[-1]
    for half in range(2):
        tables, *four = blocks[5 * half : 5 * half + 5]
        routes, gates = unpack(four)[0]
        select_rows(ids, routes, gates, 2, outs[2 * FOUR + 2 + half], select)
        select_rows(ids, tables[:TOP, :], tables[TOP:, :], FOUR, outs[2 * FOUR + half], select)
        spread(select[...], four, outs[FOUR * half : FOUR * half + FOUR])


def pick(kernel, ids, blocks, count, width, extra):
    lanes = FOUR * blocks[-1].shape[0]
    out_shape = [jax.ShapeDtypeStruct((PART, width), jnp.bfloat16)] * (FOUR * count)
    out_shape += [jax.ShapeDtypeStruct((count, lanes), dtype) for count, dtype in extra]
    outs = pl.pallas_call(
        kernel,
        out_shape=out_shape,
        in_specs=[pl.BlockSpec(memory_space=pltpu.SMEM)] + [VMEM] * len(blocks),
        out_specs=[VMEM] * len(out_shape),
        scratch_shapes=[pltpu.VMEM((FOUR * PART, lanes), jnp.bfloat16)],
        compiler_params=pltpu.CompilerParams(vmem_limit_bytes=LIMIT),
        cost_estimate=pl.CostEstimate(flops=1 << 26, bytes_accessed=1 << 20, transcendentals=0),
        name="pick",
    )(ids, *blocks)
    return list(outs[: FOUR * count]), *outs[FOUR * count :]


def pick_backward(ids, blocks, width):
    extra = [(2 * FOUR * PART, jnp.bfloat16), (2 * TOP, jnp.float32)]
    return pick(pick_backward_kernel, ids, blocks, 1, width, extra)


def pick_forward(ids, near, far, width):
    extra = [(2 * count * PART, jnp.bfloat16) for count in (FOUR, FOUR, 2, 2)]
    return pick(pick_forward_kernel, ids, (*near, *far), 2, width, extra)


def line_up(parts, j, rows):
    start = 0 if j == 0 else PART - ALIGNED
    for i, part in enumerate(parts):
        rows[i * ALIGNED : (i + 1) * ALIGNED, :] = part[start : start + ALIGNED, :]


def lay_out(results, outs):
    edge = PART // 2 // 16 * 16
    for i, out in enumerate(outs):
        at = i * ALIGNED
        out[:edge, :] = results[0, at : at + edge, :]
        low, high = results[0, at + edge : at + edge + 16, :], results[1, at : at + 16, :]
        row = lax.broadcasted_iota(jnp.int32, low.shape, 0)
        mixed = jnp.where(row < PART // 2 - edge, low.astype(jnp.float32), high.astype(jnp.float32))
        out[edge : edge + 16, :] = mixed.astype(jnp.bfloat16)
        out[edge + 16 :, :] = results[1, at + 16 : at + ALIGNED, :]


def tiles(total, tile, body):
    def step(i, _):
        body(pl.ds(pl.multiple_of(i * tile, tile), tile))
        return 0

    lax.fori_loop(0, total // tile, step, 0)


def half_rows(refs, half):
    return [ref.at[pl.ds(half * PART, PART), :] for ref in refs]


def load(weights, held, sems):
    copies = [
        pltpu.make_async_copy(array.at[j], copy.at[j], sems.at[2 * j + i])
        for j in range(2)
        for i, (array, copy) in enumerate(zip(weights, held))
    ]
    for copy in copies:
        copy.start()
    return copies


def forward_kernel(*refs):
    parts, weights, outs = refs[:FOUR], refs[FOUR : FOUR + 2], refs[FOUR + 2 : 2 * FOUR + 2]
    rows, hidden, results, w_in, w_out, sems = refs[2 * FOUR + 2 :]
    copies = load(weights, (w_in, w_out), sems)
    for j in range(2):
        line_up(parts, j, rows)

        def into(at):
            pre = jnp.dot(rows[...], w_in[j, :, at], preferred_element_type=jnp.float32)
            hidden[:, at] = (pre * jax.nn.sigmoid(pre)).astype(jnp.bfloat16)

        def outof(at):
            out = jnp.dot(hidden[...], w_out[j, :, at], preferred_element_type=jnp.float32)
            results[j, :, at] = out.astype(jnp.bfloat16)

        copies[2 * j].wait()
        tiles(hidden.shape[1], 256, into)
        copies[2 * j + 1].wait()
        tiles(rows.shape[1], 512, outof)
    lay_out(results, outs)


def backward_kernel(*refs):
    own, other, across, rows, grad_rows, hidden, results, w_in, w_out, sems = refs[10:]
    copies = load(refs[8:10], (w_in, w_out), sems)
    width = rows.shape[1]
    parts = [ref.at[:, pl.ds(0, width)] for ref in refs[:8]]
    grads = [ref.at[:, pl.ds(width, width)] for ref in refs[:8]]
    outs = []
    for half in range(2):
        outs += half_rows((own, across, other), half) + half_rows((across,), 2 + half)
    across = (((1,), (1,)), ((), ()))
    for j in range(2):
        line_up(parts, j, rows)
        line_up(grads, j, grad_rows)

        def into(at):
            pre = jnp.dot(rows[...], w_in[j, :, at], preferred_element_type=jnp.float32)
            grad = lax.dot_general(grad_rows[...], w_out[j, at, :], across, preferred_element_type=jnp.float32)
            hidden[:, at] = (grad * silu_slope(pre)).astype(jnp.bfloat16)

        def outof(at):
            out = lax.dot_general(hidden[...], w_in[j, at, :], across, preferred_element_type=jnp.float32)
            results[j, :, at] = out.astype(jnp.bfloat16)

        copies[2 * j].wait()
        copies[2 * j + 1].wait()
        tiles(hidden.shape[1], 256, into)
        tiles(rows.shape[1], 512, outof)
    lay_out(results, outs)


def experts(kernel, arrays, inputs, outs, weight_in, weight_out):
    width = weight_in.shape[1]
    rows = len(inputs) * ALIGNED
    return pl.pallas_call(
        kernel,
        out_shape=[jax.ShapeDtypeStruct((count * PART, width), jnp.bfloat16) for count in outs],
        in_specs=[VMEM] * len(inputs) + [pl.BlockSpec(memory_space=pltpu.HBM)] * 2,
        out_specs=[VMEM] * len(outs),
        scratch_shapes=[pltpu.VMEM((rows, width), jnp.bfloat16)] * arrays
        + [pltpu.VMEM((rows, weight_in.shape[2]), jnp.bfloat16), pltpu.VMEM((2, rows, width), jnp.bfloat16)]
        + [pltpu.VMEM(w.shape, jnp.bfloat16) for w in (weight_in, weight_out)]
        + [pltpu.SemaphoreType.DMA((4,))],
        compiler_params=pltpu.CompilerParams(vmem_limit_bytes=LIMIT),
        cost_estimate=pl.CostEstimate(flops=1 << 28, bytes_accessed=1 << 21, transcendentals=1 << 16),
        name="experts",
    )(*inputs, weight_in, weight_out)


def gated_kernel(half, weights, p0, p1, p2, p3, s0, s1, s2, s3, every):
    for a, part in enumerate((p0, p1, p2, p3)):
        every[a * PART : (a + 1) * PART, :] = part[half * PART : (half + 1) * PART, :]
    down = (((0,), (0,)), ((), ()))
    tokens = s0.shape[0]
    tile = 512
    for i in range(every.shape[1] // tile):
        at = slice(i * tile, (i + 1) * tile)
        total = lax.dot_general(weights[: FOUR * PART, :], every[:, at], down, preferred_element_type=jnp.float32)
        total += lax.dot_general(weights[FOUR * PART :, :], every[:, at], down, preferred_element_type=jnp.float32)
        for k, out in enumerate((s0, s1, s2, s3)):
            out[:, at] = total[k * tokens : (k + 1) * tokens].astype(jnp.bfloat16)


def gated(weights, parts, half=0):
    width = parts[0].shape[1]
    tokens = weights.shape[1] // FOUR
    return pl.pallas_call(
        functools.partial(gated_kernel, half),
        out_shape=[jax.ShapeDtypeStruct((tokens, width), jnp.bfloat16)] * FOUR,
        in_specs=[VMEM] * 5,
        out_specs=[VMEM] * FOUR,
        scratch_shapes=[pltpu.VMEM((FOUR * PART, width), jnp.bfloat16)],
        compiler_params=pltpu.CompilerParams(vmem_limit_bytes=LIMIT),
        cost_estimate=pl.CostEstimate(flops=1 << 34, bytes_accessed=1 << 22, transcendentals=0),
        name="gated",
    )(weights, *parts)


def gated_pair_kernel(half, weights, other_weights, own, other, across, s0, s1, s2, s3, every):
    pair = 2 * PART
    for i, (part, first) in enumerate(((own, half), (across, half), (other, half), (across, 2 + half))):
        every[i * PART : (i + 1) * PART, :] = part[first * PART : (first + 1) * PART, :]
    down = (((0,), (0,)), ((), ()))
    tokens = s0.shape[0] // 2
    tile = 512
    for i in range(every.shape[1] // tile):
        at = slice(i * tile, (i + 1) * tile)
        for n, (table, low) in enumerate(((weights, 2 * pair), (other_weights, pair))):
            rows = every[n * pair : (n + 1) * pair, at]
            total = lax.dot_general(table[:pair, :], rows, down, preferred_element_type=jnp.float32)
            total += lax.dot_general(table[low : low + pair, :], rows, down, preferred_element_type=jnp.float32)
            for k, out in enumerate((s0, s1, s2, s3)):
                out[n * tokens : (n + 1) * tokens, at] = total[k * tokens : (k + 1) * tokens].astype(jnp.bfloat16)


def gated_pair(half, weights, other_weights, parts):
    width = parts[0].shape[1]
    tokens = weights.shape[1] // FOUR
    return pl.pallas_call(
        functools.partial(gated_pair_kernel, half),
        out_shape=[jax.ShapeDtypeStruct((2 * tokens, width), jnp.bfloat16)] * FOUR,
        in_specs=[VMEM] * 5,
        out_specs=[VMEM] * FOUR,
        scratch_shapes=[pltpu.VMEM((FOUR * PART, width), jnp.bfloat16)],
        compiler_params=pltpu.CompilerParams(vmem_limit_bytes=LIMIT),
        cost_estimate=pl.CostEstimate(flops=4 * 320 * 256 * width, bytes_accessed=1 << 22, transcendentals=0),
        name="gated_pair",
    )(weights, other_weights, *parts)


def hop(up, down):
    return along_z(up, 1), along_z(down, -1)


def far_hop(up, down):
    half = up.shape[0] // 2
    return along_z(up[:half], 1), along_z(down[half:], -1)


def added(one, two):
    return (one.astype(jnp.float32) + two.astype(jnp.float32)).astype(jnp.bfloat16)


def turn_back(last):
    half = last.shape[0] // 2
    return along_z(last[half:], 1), along_z(last[:half], -1)


def add_halves(up, down, pair):
    half = up.shape[0] // 2
    up = jnp.concatenate([up[:half], added(up[half:], pair[0])], axis=0)
    down = jnp.concatenate([added(down[:half], pair[1]), down[half:]], axis=0)
    return up, down


def finished(base, own, others):
    total = base.astype(jnp.float32) + own.astype(jnp.float32)
    for other in others:
        total += other.astype(jnp.float32)
    return total.astype(jnp.bfloat16)


def exchange(parts):
    return [parts[0]] + [swap(parts[a], a) for a in (1, 2, 3)]


def per_device(
    fwd_input, fwd_routes, fwd_gates, bwd_input, bwd_grad, bwd_routes, bwd_gates, w_in, w_out
):
    weight_in, weight_out = w_in[0], w_out[0]
    f_own = fwd_input[0]
    width = f_own.shape[1]
    me = lax.axis_index(EXPERT)
    ids = jnp.stack([2 * (me ^ a) + j for a in range(4) for j in range(2)]).astype(jnp.int32)
    b_own, meta = pack(bwd_input[0], bwd_grad[0], fwd_routes[0], fwd_gates[0], bwd_routes[0], bwd_gates[0])

    b1 = hop(b_own, b_own)
    meta = swap(meta, 2)
    b1, meta = stage(b1, meta)
    b2 = hop(*b1)
    f_own = jnp.concatenate([f_own, meta], axis=1)
    b2, f_own = stage(b2, f_own)
    b_parts1, b_weights1, near = pick_backward(ids, (*b1, *b2), 2 * width)
    b2, b_parts1, f_own = stage(b2, b_parts1, f_own)

    b_got1 = exchange(b_parts1)
    b3 = hop(*b2)
    b4 = far_hop(*b3)
    f1 = hop(f_own, f_own)
    b_got1, b3, b4, f1 = stage(b_got1, b3, b4, f1)
    b_parts2, b_weights2, far = pick_backward(ids, (b_own, *b3, jnp.concatenate(b4, axis=0)), 2 * width)
    b_parts2, f1 = stage(b_parts2, f1)

    b_got2 = exchange(b_parts2)
    f2 = hop(*f1)
    f3 = hop(*f2)
    f4 = far_hop(*f3)
    b_got2, f2, f3, f4 = stage(b_got2, f2, f3, f4)
    f_parts, f_weights1, f_weights2, b_others1, b_others2 = pick_forward(
        ids, (near, *f1, *f2), (far, f_own, *f3, jnp.concatenate(f4, axis=0)), width
    )
    f_parts, b_got1, b_got2 = stage(f_parts, b_got1, b_got2)

    f_got2 = exchange(f_parts[4:])
    b_out = experts(backward_kernel, 2, b_got1 + b_got2, (2, 2, 4), weight_in, weight_out)
    f_got2, b_out, f_parts1 = stage(f_got2, b_out, f_parts[:4])

    f_got1 = exchange(f_parts1)
    f_out2 = experts(forward_kernel, 1, f_got2, (1,) * 4, weight_in, weight_out)
    b_out = [b_out[0], b_out[1], swap(b_out[2], 1)]
    b_sums2 = gated_pair(1, b_weights2, b_others2, b_out)
    b_pair = turn_back(b_sums2[3])
    f_got1, f_out2, b_out, b_sums2, b_pair = stage(f_got1, f_out2, b_out, b_sums2, b_pair)

    f_back2 = exchange(f_out2)
    b_pair = hop(*add_halves(b_sums2[2], b_sums2[1], b_pair))
    f_out1 = experts(forward_kernel, 1, f_got1, (1,) * 4, weight_in, weight_out)
    b_sums1 = gated_pair(0, b_weights1, b_others1, b_out)
    f_core1 = swap(f_out1[1], 1)
    f_sums2 = gated(f_weights2, f_back2)
    b_pair, f_out1, b_sums1, f_sums2, f_core1 = stage(b_pair, f_out1, b_sums1, f_sums2, f_core1)

    f_back1 = [f_out1[0], f_core1, swap(f_out1[2], 2), swap(f_out1[3], 3)]
    rows = b_sums1[0].shape[0]
    half = f_sums2[3].shape[0] // 2
    pair = hop(
        jnp.concatenate([added(b_sums1[3], b_pair[0]), f_sums2[3][half:]], axis=0),
        jnp.concatenate([added(b_sums1[2], b_pair[1]), f_sums2[3][:half]], axis=0),
    )
    f_sums1 = gated(f_weights1, f_back1)
    pair, f_sums1 = stage(pair, f_sums1)

    half = rows // 2
    f_pair = add_halves(f_sums2[2], f_sums2[1], (pair[0][rows:], pair[1][rows:]))
    b_pair = added(b_sums1[1], pair[0][:rows]), added(b_sums1[0], pair[1][:rows])
    pair = hop(*(jnp.concatenate([b[half:], f], axis=0) for b, f in zip(b_pair, f_pair)))
    pair, b_pair = stage(pair, [b[:half] for b in b_pair])

    b_other = finished(b_sums2[0][half:], pair[0][:half], (pair[1][:half],))
    b_other = swap(b_other, 2)
    f_pair = added(f_sums1[3], pair[0][half:]), added(f_sums1[2], pair[1][half:])
    pair = hop(*(jnp.concatenate([b, f], axis=0) for b, f in zip(b_pair, f_pair)))
    pair, b_other = stage(pair, b_other)

    f_pair = hop(added(f_sums1[1], pair[0][half:]), added(f_sums1[0], pair[1][half:]))
    bwd_out = finished(bwd_grad[0], b_sums2[0][:half], (pair[0][:half], pair[1][:half], b_other))
    next_cotangent = shifted(bwd_out[None], "pipe", -1)
    next_forward = shifted(finished(fwd_input[0], f_sums2[0], f_pair)[None], "pipe", 1)
    return (next_forward, next_cotangent)


def solution(mesh):
    rows = P("pipe", "expert", None)
    weights = P("pipe", "expert", None, None)
    return jax.shard_map(
        per_device,
        mesh=mesh,
        in_specs=(rows,) * 7 + (weights,) * 2,
        out_specs=(rows, rows),
        check_vma=False,
    )
```

```python
import functools

import jax
import jax.numpy as jnp
from jax import lax
from jax.experimental import pallas as pl
from jax.experimental.pallas import tpu as pltpu
from jax.sharding import PartitionSpec as P

TOP = 8
CAP = 10
EXPERT = "expert"
NEAR = (1, -1, 2, -2)
FAR = (0, 3, -3, 4)
FOUR = 4
PART = 2 * FOUR * CAP
ALIGNED = 48
META = 128
VMEM = pl.BlockSpec(memory_space=pltpu.VMEM)
LIMIT = 48 << 20


def along_z(value, by):
    count = lax.axis_size(EXPERT)
    return lax.ppermute(value, EXPERT, [(i, ((i // 4 + by) % (count // 4)) * 4 + i % 4) for i in range(count)])


def swap(value, bits):
    return lax.ppermute(value, EXPERT, [(i, i ^ bits) for i in range(lax.axis_size(EXPERT))])


def shifted(value, axis, by):
    count = lax.axis_size(axis)
    pairs = [(i, i + by) for i in range(count) if 0 <= i + by < count]
    return lax.ppermute(value, axis, pairs)


def stage(*values):
    return lax.optimization_barrier(values)


def silu_slope(values):
    sigma = jax.nn.sigmoid(values)
    return sigma * (1.0 + values * (1.0 - sigma))


def diagonal(rows):
    row = lax.broadcasted_iota(jnp.int32, (rows, META), 0)
    return jnp.where(row == lax.broadcasted_iota(jnp.int32, (rows, META), 1), 1.0, 0.0).astype(jnp.bfloat16)


def pack_kernel(x, g, f_routes, f_gates, b_routes, b_gates, out, alone, whole, fr, fg, br, bg, sems):
    width = x.shape[1]
    pairs = (
        (f_routes, fr),
        (f_gates, fg),
        (b_routes, br),
        (b_gates, bg),
        (x, whole.at[0]),
        (g, whole.at[1]),
    )
    copies = [pltpu.make_async_copy(a, b, sems.at[i]) for i, (a, b) in enumerate(pairs)]
    for copy in copies:
        copy.start()
    for copy in copies[:4]:
        copy.wait()
    rows = []
    for routes, gates in ((br, bg), (fr, fg)):
        rows.append(routes[...].astype(jnp.float32))
        rest = gates[...]
        for _ in range(3):
            part = rest.astype(jnp.bfloat16).astype(jnp.float32)
            rows.append(part)
            rest = rest - part
    table = jnp.concatenate(rows, axis=0).astype(jnp.bfloat16)
    meta = lax.dot_general(
        table, diagonal(8 * TOP), (((0,), (0,)), ((), ())), preferred_element_type=jnp.float32
    )
    out[:, 2 * width :] = meta.astype(jnp.bfloat16)
    alone[...] = meta.astype(jnp.bfloat16)
    for i, copy in enumerate(copies[4:]):
        copy.wait()
        out[:, i * width : (i + 1) * width] = whole[i]


def pack(x, g, f_routes, f_gates, b_routes, b_gates):
    return pl.pallas_call(
        pack_kernel,
        out_shape=[
            jax.ShapeDtypeStruct((x.shape[0], columns), jnp.bfloat16) for columns in (2 * x.shape[1] + META, META)
        ],
        in_specs=[pl.BlockSpec(memory_space=pl.ANY)] * 6,
        out_specs=[VMEM] * 2,
        scratch_shapes=[pltpu.VMEM((2, *x.shape), jnp.bfloat16)]
        + [pltpu.VMEM((TOP, x.shape[0]), dtype) for dtype in (jnp.int32, jnp.float32) * 2]
        + [pltpu.SemaphoreType.DMA((6,))],
        compiler_params=pltpu.CompilerParams(vmem_limit_bytes=60 << 20),
        name="pack",
    )(x, g, f_routes.T, f_gates.T, b_routes.T, b_gates.T)


def unpack(blocks):
    meta = jnp.concatenate([b[:, b.shape[1] - META :] for b in blocks], axis=0)
    rows = lax.dot_general(
        diagonal(8 * TOP), meta, (((1,), (1,)), ((), ())), preferred_element_type=jnp.float32
    )
    both = []
    for start in (0, 4 * TOP):
        part = [rows[start + i * TOP : start + (i + 1) * TOP] for i in range(4)]
        both.append((part[0], part[1] + part[2] + part[3]))
    return both


def select_rows(ids, routes, gates, count, weights, select):
    lanes = routes.shape[1]
    tokens = lanes // FOUR
    row = lax.broadcasted_iota(jnp.int32, (2 * FOUR, lanes), 0)
    named = jnp.zeros((2 * FOUR, lanes), jnp.float32)
    gate = jnp.zeros((2 * FOUR, lanes), jnp.float32)
    for x in range(2 * FOUR):
        hit = routes == ids[x].astype(jnp.float32)
        named = jnp.where(row == x, jnp.max(jnp.where(hit, 1.0, 0.0), axis=0, keepdims=True), named)
        gate = jnp.where(row == x, jnp.sum(jnp.where(hit, gates, 0.0), axis=0, keepdims=True), gate)
    first = lax.broadcasted_iota(jnp.int32, (lanes, lanes), 0)
    second = lax.broadcasted_iota(jnp.int32, (lanes, lanes), 1)
    before = jnp.where((first < second) & (first // tokens == second // tokens), 1.0, 0.0).astype(jnp.bfloat16)
    position = jnp.dot(named.astype(jnp.bfloat16), before, preferred_element_type=jnp.float32)
    source = lax.broadcasted_iota(jnp.int32, (2 * FOUR, lanes), 1) // tokens
    slot = jnp.where(named > 0.5, position + (source * CAP).astype(jnp.float32), -1.0)
    place = lax.broadcasted_iota(jnp.int32, (PART, lanes), 0)
    early = place < PART // 2
    place = jnp.where(early, place, place - PART // 2).astype(jnp.float32)
    for a in range(count):
        match = jnp.where(early, slot[2 * a : 2 * a + 1], slot[2 * a + 1 : 2 * a + 2]) == place
        weight = jnp.where(match, jnp.where(early, gate[2 * a : 2 * a + 1], gate[2 * a + 1 : 2 * a + 2]), 0.0)
        high = weight.astype(jnp.bfloat16)
        select[a * PART : (a + 1) * PART, :] = jnp.where(match, 1.0, 0.0).astype(jnp.bfloat16)
        weights[a * PART : (a + 1) * PART, :] = high
        weights[(count + a) * PART : (count + a + 1) * PART, :] = (weight - high.astype(jnp.float32)).astype(jnp.bfloat16)


def spread(chosen, four, outs):
    tile = 512
    for i in range(outs[0].shape[1] // tile):
        at = slice(i * tile, (i + 1) * tile)
        block = jnp.concatenate([b[:, at] for b in four], axis=0)
        slots = jnp.dot(chosen, block, preferred_element_type=jnp.float32)
        for a in range(FOUR):
            outs[a][:, at] = slots[a * PART : (a + 1) * PART].astype(jnp.bfloat16)


def pick_backward_kernel(ids, b0, b1, b2, b3, p0, p1, p2, p3, weights, tables, select):
    blocks = (b0, b1, b2, b3)
    (routes, gates), (other_routes, other_gates) = unpack(blocks)
    tables[:TOP, :] = other_routes
    tables[TOP:, :] = other_gates
    select_rows(ids, routes, gates, FOUR, weights, select)
    spread(select[...], blocks, (p0, p1, p2, p3))


def pick_forward_kernel(ids, *refs):
    blocks, outs, select = refs[:10], refs[10:-1], refs[-1]
    for half in range(2):
        tables, *four = blocks[5 * half : 5 * half + 5]
        routes, gates = unpack(four)[0]
        select_rows(ids, routes, gates, 2, outs[2 * FOUR + 2 + half], select)
        select_rows(ids, tables[:TOP, :], tables[TOP:, :], FOUR, outs[2 * FOUR + half], select)
        spread(select[...], four, outs[FOUR * half : FOUR * half + FOUR])


def pick(kernel, ids, blocks, count, width, extra):
    lanes = FOUR * blocks[-1].shape[0]
    out_shape = [jax.ShapeDtypeStruct((PART, width), jnp.bfloat16)] * (FOUR * count)
    out_shape += [jax.ShapeDtypeStruct((count, lanes), dtype) for count, dtype in extra]
    outs = pl.pallas_call(
        kernel,
        out_shape=out_shape,
        in_specs=[pl.BlockSpec(memory_space=pltpu.SMEM)] + [VMEM] * len(blocks),
        out_specs=[VMEM] * len(out_shape),
        scratch_shapes=[pltpu.VMEM((FOUR * PART, lanes), jnp.bfloat16)],
        compiler_params=pltpu.CompilerParams(vmem_limit_bytes=LIMIT),
        cost_estimate=pl.CostEstimate(flops=1 << 26, bytes_accessed=1 << 20, transcendentals=0),
        name="pick",
    )(ids, *blocks)
    return list(outs[: FOUR * count]), *outs[FOUR * count :]


def pick_backward(ids, blocks, width):
    extra = [(2 * FOUR * PART, jnp.bfloat16), (2 * TOP, jnp.float32)]
    return pick(pick_backward_kernel, ids, blocks, 1, width, extra)


def pick_forward(ids, near, far, width):
    extra = [(2 * count * PART, jnp.bfloat16) for count in (FOUR, FOUR, 2, 2)]
    return pick(pick_forward_kernel, ids, (*near, *far), 2, width, extra)


def line_up(parts, j, rows):
    start = 0 if j == 0 else PART - ALIGNED
    for i, part in enumerate(parts):
        rows[i * ALIGNED : (i + 1) * ALIGNED, :] = part[start : start + ALIGNED, :]


def lay_out(results, outs):
    edge = PART // 2 // 16 * 16
    for i, out in enumerate(outs):
        at = i * ALIGNED
        out[:edge, :] = results[0, at : at + edge, :]
        low, high = results[0, at + edge : at + edge + 16, :], results[1, at : at + 16, :]
        row = lax.broadcasted_iota(jnp.int32, low.shape, 0)
        mixed = jnp.where(row < PART // 2 - edge, low.astype(jnp.float32), high.astype(jnp.float32))
        out[edge : edge + 16, :] = mixed.astype(jnp.bfloat16)
        out[edge + 16 :, :] = results[1, at + 16 : at + ALIGNED, :]


def tiles(total, tile, body):
    def step(i, _):
        body(pl.ds(pl.multiple_of(i * tile, tile), tile))
        return 0

    lax.fori_loop(0, total // tile, step, 0)


def half_rows(refs, half):
    return [ref.at[pl.ds(half * PART, PART), :] for ref in refs]


def load(weights, held, sems):
    copies = [
        pltpu.make_async_copy(array.at[j], copy.at[j], sems.at[2 * j + i])
        for j in range(2)
        for i, (array, copy) in enumerate(zip(weights, held))
    ]
    for copy in copies:
        copy.start()
    return copies


def forward_kernel(*refs):
    parts, weights, outs = refs[:FOUR], refs[FOUR : FOUR + 2], refs[FOUR + 2 : 2 * FOUR + 2]
    rows, hidden, results, w_in, w_out, sems = refs[2 * FOUR + 2 :]
    copies = load(weights, (w_in, w_out), sems)
    for j in range(2):
        line_up(parts, j, rows)

        def into(at):
            pre = jnp.dot(rows[...], w_in[j, :, at], preferred_element_type=jnp.float32)
            hidden[:, at] = (pre * jax.nn.sigmoid(pre)).astype(jnp.bfloat16)

        def outof(at):
            out = jnp.dot(hidden[...], w_out[j, :, at], preferred_element_type=jnp.float32)
            results[j, :, at] = out.astype(jnp.bfloat16)

        copies[2 * j].wait()
        tiles(hidden.shape[1], 256, into)
        copies[2 * j + 1].wait()
        tiles(rows.shape[1], 512, outof)
    lay_out(results, outs)


def backward_kernel(*refs):
    own, other, across, rows, grad_rows, hidden, results, w_in, w_out, sems = refs[10:]
    copies = load(refs[8:10], (w_in, w_out), sems)
    width = rows.shape[1]
    parts = [ref.at[:, pl.ds(0, width)] for ref in refs[:8]]
    grads = [ref.at[:, pl.ds(width, width)] for ref in refs[:8]]
    outs = []
    for half in range(2):
        outs += half_rows((own, across, other), half) + half_rows((across,), 2 + half)
    across = (((1,), (1,)), ((), ()))
    for j in range(2):
        line_up(parts, j, rows)
        line_up(grads, j, grad_rows)

        def into(at):
            pre = jnp.dot(rows[...], w_in[j, :, at], preferred_element_type=jnp.float32)
            grad = lax.dot_general(grad_rows[...], w_out[j, at, :], across, preferred_element_type=jnp.float32)
            hidden[:, at] = (grad * silu_slope(pre)).astype(jnp.bfloat16)

        def outof(at):
            out = lax.dot_general(hidden[...], w_in[j, at, :], across, preferred_element_type=jnp.float32)
            results[j, :, at] = out.astype(jnp.bfloat16)

        copies[2 * j].wait()
        copies[2 * j + 1].wait()
        tiles(hidden.shape[1], 256, into)
        tiles(rows.shape[1], 512, outof)
    lay_out(results, outs)


def experts(kernel, arrays, inputs, outs, weight_in, weight_out):
    width = weight_in.shape[1]
    rows = len(inputs) * ALIGNED
    return pl.pallas_call(
        kernel,
        out_shape=[jax.ShapeDtypeStruct((count * PART, width), jnp.bfloat16) for count in outs],
        in_specs=[VMEM] * len(inputs) + [pl.BlockSpec(memory_space=pltpu.HBM)] * 2,
        out_specs=[VMEM] * len(outs),
        scratch_shapes=[pltpu.VMEM((rows, width), jnp.bfloat16)] * arrays
        + [pltpu.VMEM((rows, weight_in.shape[2]), jnp.bfloat16), pltpu.VMEM((2, rows, width), jnp.bfloat16)]
        + [pltpu.VMEM(w.shape, jnp.bfloat16) for w in (weight_in, weight_out)]
        + [pltpu.SemaphoreType.DMA((4,))],
        compiler_params=pltpu.CompilerParams(vmem_limit_bytes=LIMIT),
        cost_estimate=pl.CostEstimate(flops=1 << 28, bytes_accessed=1 << 21, transcendentals=1 << 16),
        name="experts",
    )(*inputs, weight_in, weight_out)


def gated_kernel(half, weights, p0, p1, p2, p3, s0, s1, s2, s3, every):
    for a, part in enumerate((p0, p1, p2, p3)):
        every[a * PART : (a + 1) * PART, :] = part[half * PART : (half + 1) * PART, :]
    down = (((0,), (0,)), ((), ()))
    tokens = s0.shape[0]
    tile = 512
    for i in range(every.shape[1] // tile):
        at = slice(i * tile, (i + 1) * tile)
        total = lax.dot_general(weights[: FOUR * PART, :], every[:, at], down, preferred_element_type=jnp.float32)
        total += lax.dot_general(weights[FOUR * PART :, :], every[:, at], down, preferred_element_type=jnp.float32)
        for k, out in enumerate((s0, s1, s2, s3)):
            out[:, at] = total[k * tokens : (k + 1) * tokens].astype(jnp.bfloat16)


def gated(weights, parts, half=0):
    width = parts[0].shape[1]
    tokens = weights.shape[1] // FOUR
    return pl.pallas_call(
        functools.partial(gated_kernel, half),
        out_shape=[jax.ShapeDtypeStruct((tokens, width), jnp.bfloat16)] * FOUR,
        in_specs=[VMEM] * 5,
        out_specs=[VMEM] * FOUR,
        scratch_shapes=[pltpu.VMEM((FOUR * PART, width), jnp.bfloat16)],
        compiler_params=pltpu.CompilerParams(vmem_limit_bytes=LIMIT),
        cost_estimate=pl.CostEstimate(flops=1 << 34, bytes_accessed=1 << 22, transcendentals=0),
        name="gated",
    )(weights, *parts)


def gated_pair_kernel(half, weights, other_weights, own, other, across, s0, s1, s2, s3, every):
    pair = 2 * PART
    for i, (part, first) in enumerate(((own, half), (across, half), (other, half), (across, 2 + half))):
        every[i * PART : (i + 1) * PART, :] = part[first * PART : (first + 1) * PART, :]
    down = (((0,), (0,)), ((), ()))
    tokens = s0.shape[0] // 2
    tile = 512
    for i in range(every.shape[1] // tile):
        at = slice(i * tile, (i + 1) * tile)
        for n, (table, low) in enumerate(((weights, 2 * pair), (other_weights, pair))):
            rows = every[n * pair : (n + 1) * pair, at]
            total = lax.dot_general(table[:pair, :], rows, down, preferred_element_type=jnp.float32)
            total += lax.dot_general(table[low : low + pair, :], rows, down, preferred_element_type=jnp.float32)
            for k, out in enumerate((s0, s1, s2, s3)):
                out[n * tokens : (n + 1) * tokens, at] = total[k * tokens : (k + 1) * tokens].astype(jnp.bfloat16)


def gated_pair(half, weights, other_weights, parts):
    width = parts[0].shape[1]
    tokens = weights.shape[1] // FOUR
    return pl.pallas_call(
        functools.partial(gated_pair_kernel, half),
        out_shape=[jax.ShapeDtypeStruct((2 * tokens, width), jnp.bfloat16)] * FOUR,
        in_specs=[VMEM] * 5,
        out_specs=[VMEM] * FOUR,
        scratch_shapes=[pltpu.VMEM((FOUR * PART, width), jnp.bfloat16)],
        compiler_params=pltpu.CompilerParams(vmem_limit_bytes=LIMIT),
        cost_estimate=pl.CostEstimate(flops=4 * 320 * 256 * width, bytes_accessed=1 << 22, transcendentals=0),
        name="gated_pair",
    )(weights, other_weights, *parts)


def hop(up, down):
    return along_z(up, 1), along_z(down, -1)


def far_hop(up, down):
    half = up.shape[0] // 2
    return along_z(up[:half], 1), along_z(down[half:], -1)


def added(one, two):
    return (one.astype(jnp.float32) + two.astype(jnp.float32)).astype(jnp.bfloat16)


def turn_back(last):
    half = last.shape[0] // 2
    return along_z(last[half:], 1), along_z(last[:half], -1)


def add_halves(up, down, pair):
    half = up.shape[0] // 2
    up = jnp.concatenate([up[:half], added(up[half:], pair[0])], axis=0)
    down = jnp.concatenate([added(down[:half], pair[1]), down[half:]], axis=0)
    return up, down


def finished(base, own, others):
    total = base.astype(jnp.float32) + own.astype(jnp.float32)
    for other in others:
        total += other.astype(jnp.float32)
    return total.astype(jnp.bfloat16)


def settle_kernel(value, out):
    out[...] = value[...]


def settle(value):
    return pl.pallas_call(
        settle_kernel,
        out_shape=jax.ShapeDtypeStruct(value.shape, value.dtype),
        in_specs=[VMEM],
        out_specs=VMEM,
        compiler_params=pltpu.CompilerParams(vmem_limit_bytes=LIMIT),
        cost_estimate=pl.CostEstimate(flops=1 << 20, bytes_accessed=1 << 19, transcendentals=0),
        name="settle",
    )(value)


def exchange(parts):
    return [parts[0]] + [swap(parts[a], a) for a in (1, 2, 3)]


def per_device(
    fwd_input, fwd_routes, fwd_gates, bwd_input, bwd_grad, bwd_routes, bwd_gates, w_in, w_out
):
    weight_in, weight_out = w_in[0], w_out[0]
    f_own = fwd_input[0]
    width = f_own.shape[1]
    me = lax.axis_index(EXPERT)
    ids = jnp.stack([2 * (me ^ a) + j for a in range(4) for j in range(2)]).astype(jnp.int32)
    b_own, meta = pack(bwd_input[0], bwd_grad[0], fwd_routes[0], fwd_gates[0], bwd_routes[0], bwd_gates[0])

    b1 = hop(b_own, b_own)
    meta = swap(meta, 2)
    b1, meta = stage(b1, meta)
    b2 = hop(*b1)
    f_own = jnp.concatenate([f_own, meta], axis=1)
    b2, f_own = stage(b2, f_own)
    b_parts1, b_weights1, near = pick_backward(ids, (*b1, *b2), 2 * width)
    b2, b_parts1, f_own = stage(b2, b_parts1, f_own)

    b_got1 = exchange(b_parts1)
    b3 = hop(*b2)
    b4 = far_hop(*b3)
    f1 = hop(f_own, f_own)
    b_got1, b3, b4, f1 = stage(b_got1, b3, b4, f1)
    b_parts2, b_weights2, far = pick_backward(ids, (b_own, *b3, jnp.concatenate(b4, axis=0)), 2 * width)
    b_parts2, f1 = stage(b_parts2, f1)

    b_got2 = exchange(b_parts2)
    f2 = hop(*f1)
    f3 = hop(*f2)
    f4 = far_hop(*f3)
    b_got2, f2, f3, f4 = stage(b_got2, f2, f3, f4)
    f_parts, f_weights1, f_weights2, b_others1, b_others2 = pick_forward(
        ids, (near, *f1, *f2), (far, f_own, *f3, jnp.concatenate(f4, axis=0)), width
    )
    f_parts, b_got1, b_got2 = stage(f_parts, b_got1, b_got2)

    f_got2 = exchange(f_parts[4:])
    b_out = experts(backward_kernel, 2, b_got1 + b_got2, (2, 2, 4), weight_in, weight_out)
    f_got2, b_out, f_parts1 = stage(f_got2, b_out, f_parts[:4])

    f_got1 = exchange(f_parts1)
    f_out2 = experts(forward_kernel, 1, f_got2, (1,) * 4, weight_in, weight_out)
    b_out = [b_out[0], b_out[1], swap(b_out[2], 1)]
    b_sums2 = gated_pair(1, b_weights2, b_others2, b_out)
    b_pair = turn_back(b_sums2[3])
    f_got1, f_out2, b_out, b_sums2, b_pair = stage(f_got1, f_out2, b_out, b_sums2, b_pair)

    f_back2 = exchange(f_out2)
    b_pair = hop(*add_halves(b_sums2[2], b_sums2[1], b_pair))
    f_out1 = experts(forward_kernel, 1, f_got1, (1,) * 4, weight_in, weight_out)
    b_sums1 = gated_pair(0, b_weights1, b_others1, b_out)
    f_core1 = swap(f_out1[1], 1)
    f_sums2 = gated(f_weights2, f_back2)
    b_pair, f_out1, b_sums1, f_sums2, f_core1 = stage(b_pair, f_out1, b_sums1, f_sums2, f_core1)

    f_back1 = [f_out1[0], f_core1, swap(f_out1[2], 2), swap(f_out1[3], 3)]
    rows = b_sums1[0].shape[0]
    half = f_sums2[3].shape[0] // 2
    pair = hop(
        jnp.concatenate([added(b_sums1[3], b_pair[0]), f_sums2[3][half:]], axis=0),
        jnp.concatenate([added(b_sums1[2], b_pair[1]), f_sums2[3][:half]], axis=0),
    )
    f_sums1 = gated(f_weights1, f_back1)
    pair, f_sums1 = stage(pair, f_sums1)

    half = rows // 2
    f_pair = add_halves(f_sums2[2], f_sums2[1], (pair[0][rows:], pair[1][rows:]))
    b_pair = added(b_sums1[1], pair[0][:rows]), added(b_sums1[0], pair[1][:rows])
    pair = hop(*(jnp.concatenate([b[half:], f], axis=0) for b, f in zip(b_pair, f_pair)))
    pair, b_pair = stage(pair, [b[:half] for b in b_pair])

    b_other = finished(b_sums2[0][half:], pair[0][:half], (pair[1][:half],))
    b_other = swap(b_other, 2)
    f_pair = added(f_sums1[3], pair[0][half:]), added(f_sums1[2], pair[1][half:])
    pair = hop(*(jnp.concatenate([b, f], axis=0) for b, f in zip(b_pair, f_pair)))
    pair, b_other = stage(pair, b_other)

    f_pair = hop(added(f_sums1[1], pair[0][half:]), added(f_sums1[0], pair[1][half:]))
    bwd_out = finished(bwd_grad[0], b_sums2[0][:half], (pair[0][:half], pair[1][:half], b_other))
    next_cotangent = settle(shifted(bwd_out[None], "pipe", -1))
    next_forward = shifted(finished(fwd_input[0], f_sums2[0], f_pair)[None], "pipe", 1)
    return (next_forward, next_cotangent)


def solution(mesh):
    rows = P("pipe", "expert", None)
    weights = P("pipe", "expert", None, None)
    return jax.shard_map(
        per_device,
        mesh=mesh,
        in_specs=(rows,) * 7 + (weights,) * 2,
        out_specs=(rows, rows),
        check_vma=False,
    )
```
